128 devices in a mesh: node: 8 (over x_hi, y), local: 16 (over z, x_lo, core).
Axes of the slice: x: 4 (x_hi: 2, x_lo: 2; x = x_hi * 2 + x_lo), y: 4, z: 4, core: 2. Of those that a mesh axis runs over, the one named last changes fastest.
Arguments:
- activations: bfloat16 [49152, 1024], P(('node', 'local')), may hold values from -6 to 6
- cotangent: bfloat16 [49152, 1024], P(('node', 'local')), may hold values from -4 to 4
- gate_up: bfloat16 [3072, 2, 1024], P(('node', 'local')), may hold values from -0.109375 to 0.109375
- down_proj: bfloat16 [3072, 1024], P(('node', 'local')), may hold values from -0.1875 to 0.1875
Outputs:
- grad_input: bfloat16 [49152, 1024], P(('node', 'local'))
- grad_weights: float32 [3072, 3, 1024], P(('node', 'local'))
The draws below stay inside these ranges and needn't reach their ends.
All inputs are finite; a program needn't handle non-finite values. Where the reference program divides by a largest or mean magnitude, that divisor is 1e-20 or more.
Results may differ from the reference program's by a relative error of at most 0.014.
Values may be sent and summed in bfloat16 or wider, within the bound.
No kernel may reach another device: no remote copies, remote signals or barrier semaphores. Data moves between devices by JAX's collectives and lax.ppermute only.
A program may use at most 320 MiB of HBM per device.

```python
import jax
import jax.numpy as jnp
from jax import lax

D = 1024
FF = 3072
TOK_DEV = 384
TOKENS = 49152
N_NODE = 8
N_LOCAL = 16


def level_of(key, shape, pieces, low, largest):
    level = 1.0
    for dim, parts in pieces:
        heights = jax.random.uniform(jax.random.fold_in(jax.random.fold_in(key, 6), dim), (parts,), jnp.float32, low / len(pieces), largest / len(pieces))
        level = level * jnp.repeat(jnp.exp(heights), shape[dim] // parts).reshape((-1,) + (1,) * (len(shape) - 1 - dim))
    return level


def scatter_about(rng, shape, deviation, limit, cuts=(), kind=jnp.bfloat16):
    drawn = jax.random.normal(rng, shape, jnp.float32) * deviation
    if len(cuts) > 0:
        drawn = level_of(rng, shape, cuts, -0.22, 0.18) * drawn
    return jnp.clip(drawn, min=-limit, max=limit).astype(kind)


def setup_inputs(seed: int = 0) -> dict:
    key_list = jax.random.split(jax.random.key(seed), 5)
    return {
        "activations": scatter_about(key_list[0], (TOKENS, D), ((FF / D) ** 0.5), 6.0, ((0, 128),)),
        "cotangent": scatter_about(key_list[1], (TOKENS, D), 0.25, 4.0, ((0, 128),)),
        "gate_up": scatter_about(key_list[2], (FF, 2, D), FF ** -0.5, 0.109375, ((0, 128),)),
        "down_proj": scatter_about(key_list[3], (FF, D), D ** -0.5, 0.1875, ((0, 128),)),
    }


EPS = 1e-6


def quantize(values):
    layout = values.shape
    blocks = values.reshape(layout[:-1] + (layout[-1] // 128, 128))
    scales = (jnp.max(jnp.abs(blocks), axis=-1) + EPS).astype(jnp.bfloat16)
    levels = (blocks / scales.astype(jnp.float32)[..., None]).astype(jnp.bfloat16)
    return levels.reshape(layout), scales


def restore(levels, scales):
    layout = levels.shape
    blocks = levels.astype(jnp.float32).reshape(layout[:-1] + (layout[-1] // 128, 128))
    return (blocks * scales.astype(jnp.float32)[..., None]).reshape(layout)


def unit_terms(activations, cotangent, gate_rows, up_rows, down_rows):
    gate_value = jnp.dot(activations, gate_rows.T, preferred_element_type=jnp.float32)
    upward = jnp.dot(activations, up_rows.T, preferred_element_type=jnp.float32)
    grad_hidden = jnp.dot(cotangent, down_rows.T, preferred_element_type=jnp.float32)
    sigmoid_gate = jax.nn.sigmoid(gate_value)
    silu_gate = gate_value * sigmoid_gate
    hidden = (silu_gate * upward).astype(jnp.bfloat16)
    silu_slope = sigmoid_gate * (1.0 + gate_value * (1.0 - sigmoid_gate))
    grad_gate = (grad_hidden * upward * silu_slope).astype(jnp.bfloat16)
    grad_up = (grad_hidden * silu_gate).astype(jnp.bfloat16)
    return hidden, grad_gate, grad_up


def reference(activations, cotangent, gate_up, down_proj):
    hidden, grad_gate, grad_up = unit_terms(activations, cotangent, gate_up[:, 0], gate_up[:, 1], down_proj)
    input_sum = jnp.dot(grad_gate, gate_up[:, 0], preferred_element_type=jnp.float32)
    input_sum = input_sum + jnp.dot(grad_up, gate_up[:, 1], preferred_element_type=jnp.float32)
    grad_input = input_sum.astype(jnp.bfloat16)

    def device_partial(device_index):
        row_start = (device_index * TOK_DEV).astype(jnp.int32)
        rows_act = lax.dynamic_slice_in_dim(activations, row_start, TOK_DEV, 0)
        rows_cot = lax.dynamic_slice_in_dim(cotangent, row_start, TOK_DEV, 0)
        rows_hid = lax.dynamic_slice_in_dim(hidden, row_start, TOK_DEV, 0)
        rows_gate = lax.dynamic_slice_in_dim(grad_gate, row_start, TOK_DEV, 0)
        rows_up = lax.dynamic_slice_in_dim(grad_up, row_start, TOK_DEV, 0)
        return jnp.stack([
            jnp.dot(rows_gate.T, rows_act, preferred_element_type=jnp.float32),
            jnp.dot(rows_up.T, rows_act, preferred_element_type=jnp.float32),
            jnp.dot(rows_hid.T, rows_cot, preferred_element_type=jnp.float32)], axis=1)

    def node_step(grand_total, node_index):
        def local_step(node_sum, local_index):
            levels, scales = quantize(device_partial(node_index * N_LOCAL + local_index))
            return node_sum + restore(levels, scales), None

        node_sum, _ = lax.scan(local_step, jnp.zeros((FF, 3, D), jnp.float32), jnp.arange(N_LOCAL, dtype=jnp.int32))
        levels, scales = quantize(node_sum)
        return grand_total + restore(levels, scales), None

    grad_weights, _ = lax.scan(node_step, jnp.zeros((FF, 3, D), jnp.float32), jnp.arange(N_NODE, dtype=jnp.int32))
    return grad_input, grad_weights
```

```python
import jax
import jax.numpy as jnp
from jax import lax
from jax.experimental import pallas as pl
from jax.experimental.pallas import tpu as pltpu
from jax.sharding import PartitionSpec as P

AXES = ("node", "local")
RING = 4
BF16 = jnp.bfloat16
F32 = jnp.float32


def place(device):
    x_hi, y, z, x_lo, core = device // 64, device // 16 % 4, device // 4 % 4, device // 2 % 2, device % 2
    return [x_hi * 2 + x_lo, y, z, core]


def index(x, y, z, core):
    return (x // 2) * 64 + y * 16 + z * 4 + (x % 2) * 2 + core


def partner(axis, kind):
    pairs = []
    for device in range(128):
        there = place(device)
        i = there[axis]
        if kind == "up":
            there[axis] = (i + 1) % RING
        elif kind == "down":
            there[axis] = (i - 1) % RING
        elif kind == "near":
            there[axis] = i ^ 1
        elif kind == "wrap":
            there[axis] = RING - 1 - i
        pairs.append((device, index(*there)))
    return pairs


def send(value, axis, kind):
    return lax.ppermute(value, AXES, partner(axis, kind))


def joined(first, second):
    a, b = first.shape[0] * 2 // 3, second.shape[0] * 2 // 3
    return jnp.concatenate([first[:a], second[:b], first[a:], second[b:]], axis=0)


def parted(both):
    n = both.shape[0] // 2
    a = n * 2 // 3
    return (
        jnp.concatenate([both[:a], both[2 * a : 2 * a + n - a]], axis=0),
        jnp.concatenate([both[a : 2 * a], both[2 * a + n - a :]], axis=0),
    )


def gather_plane(message, first, second):
    near = send(message, first, "near")
    half0 = joined(message, near)
    half1 = send(half0, first, "wrap")
    quarter0 = joined(half0, send(half0, second, "near"))
    quarter2 = joined(half1, send(half1, second, "wrap"))
    quarter1 = send(quarter0, second, "wrap")
    quarter3 = send(quarter2, second, "near")
    return jnp.stack([quarter0, quarter1, quarter2, quarter3])


def add(a, b):
    return (a.astype(F32) + b.astype(F32)).astype(BF16)


def reduce_plane(block, first, second):
    quarter0 = add(block[0], send(block[1], second, "wrap"))
    quarter2 = add(block[2], send(block[3], second, "near"))
    keep0, give0 = parted(quarter0)
    keep2, give2 = parted(quarter2)
    half0 = add(keep0, send(give0, second, "near"))
    half1 = add(keep2, send(give2, second, "wrap"))
    half0 = add(half0, send(half1, first, "wrap"))
    keep, give = parted(half0)
    return keep.astype(F32) + send(give, first, "near").astype(F32)


def units_kernel(has_acc, is_last, n, *refs):
    x_ref, c_ref = refs[:2]
    refs = refs[2:]
    if has_acc:
        acc_ref, refs = refs[0], refs[1:]
    blocks, refs = refs[:n], refs[n:]
    grads, refs = refs[:n], refs[n:]
    quarters = blocks[0].shape[0]
    x = x_ref[...]
    c = c_ref[...]
    tokens = x.shape[0]
    gu = jnp.concatenate([b[q, :64] for b in blocks for q in range(quarters)], axis=0)
    down = jnp.concatenate([b[q, 64:] for b in blocks for q in range(quarters)], axis=0)
    nt = (((1,), (1,)), ((), ()))
    tn = (((0,), (0,)), ((), ()))
    z = lax.dot_general(gu, x, nt, preferred_element_type=F32)
    z = z.reshape(-1, 2, 8, tokens)
    gate, up = z[:, 0], z[:, 1]
    gh = lax.dot_general(down, c, nt, preferred_element_type=F32).reshape(-1, 8, tokens)
    sg = 1.0 / (1.0 + jnp.exp(-gate))
    silu = gate * sg
    hidden = silu * up
    grad_gate = gh * up * sg * (1.0 + gate * (1.0 - sg))
    grad_up = gh * silu
    a = jnp.stack([grad_gate, grad_up], axis=1).reshape(-1, tokens).astype(BF16)
    hidden = hidden.reshape(-1, tokens).astype(BF16)
    d_gu = jnp.dot(a, x, preferred_element_type=F32).astype(BF16)
    d_down = jnp.dot(hidden, c, preferred_element_type=F32).astype(BF16)
    i = 0
    for g in grads:
        for q in range(quarters):
            g[q, :64] = d_gu[i * 64 : (i + 1) * 64]
            g[q, 64:] = d_down[i * 32 : (i + 1) * 32]
            i += 1
    acc = lax.dot_general(a, gu, tn, preferred_element_type=F32)
    if has_acc:
        acc = acc + acc_ref[...]
    if is_last:
        own_ref, other_ref = refs
        own_ref[...] = acc[: tokens // 2]
        other_ref[...] = acc[tokens // 2 :].astype(BF16)
    else:
        refs[0][...] = acc


def units(x, c, acc, blocks, is_last=False):
    tokens, width = x.shape
    outs = [jax.ShapeDtypeStruct(b.shape, BF16) for b in blocks]
    if is_last:
        outs += [
            jax.ShapeDtypeStruct((tokens // 2, width), F32),
            jax.ShapeDtypeStruct((tokens // 2, width), BF16),
        ]
    else:
        outs += [jax.ShapeDtypeStruct((tokens, width), F32)]
    count = sum(b.size for b in blocks) // (3 * width)
    args = [x, c] + ([] if acc is None else [acc]) + list(blocks)

    def body(*refs):
        units_kernel(acc is not None, is_last, len(blocks), *refs)

    return pl.pallas_call(
        body,
        out_shape=outs,
        in_specs=[pl.BlockSpec(memory_space=pltpu.VMEM)] * len(args),
        out_specs=[pl.BlockSpec(memory_space=pltpu.VMEM)] * len(outs),
        compiler_params=pltpu.CompilerParams(vmem_limit_bytes=48 * 1024 * 1024),
        cost_estimate=pl.CostEstimate(
            flops=16 * tokens * width * count,
            bytes_accessed=2 * (2 * tokens * width + 6 * count * width) + 8 * tokens * width,
            transcendentals=2 * tokens * count,
        ),
    )(*args)


def body(activations, cotangent, gate_up, down_proj):
    width = activations.shape[1]
    pair = [(d, d ^ 1) for d in range(128)]
    x = jnp.concatenate([activations, lax.ppermute(activations, AXES, pair)], axis=0)
    c = jnp.concatenate([cotangent, lax.ppermute(cotangent, AXES, pair)], axis=0)
    orders = [(0, 1, 2), (1, 2, 0), (2, 0, 1)]
    planes = []
    for p, (first, second, _) in enumerate(orders):
        rows = slice(8 * p, 8 * p + 8)
        message = jnp.concatenate([gate_up[rows, 0], gate_up[rows, 1], down_proj[rows]], axis=0)
        planes.append(gather_plane(message, first, second))
    below = [send(b, o[2], "up") for b, o in zip(planes, orders)]
    above = [send(b, o[2], "down") for b, o in zip(planes, orders)]
    far0 = [send(b[:2], o[2], "up") for b, o in zip(below, orders)]
    far1 = [send(b[2:], o[2], "down") for b, o in zip(above, orders)]

    *g_own, acc = units(x, c, None, planes)
    *g_below, acc = units(x, c, acc, below)
    *g_above, acc = units(x, c, acc, above)
    *g_far, own_sum, other_sum = units(x, c, acc, far0 + far1, is_last=True)

    grad_input = (own_sum + lax.ppermute(other_sum, AXES, pair).astype(F32)).astype(BF16)

    rows = []
    for p, (first, second, last) in enumerate(orders):
        from_above = send(g_far[p], last, "down")
        from_below = send(g_far[3 + p], last, "up")
        to_below = jnp.concatenate([add(g_below[p][:2], from_above), g_below[p][2:]], axis=0)
        to_above = jnp.concatenate([g_above[p][:2], add(g_above[p][2:], from_below)], axis=0)
        block = (
            g_own[p].astype(F32)
            + send(to_below, last, "down").astype(F32)
            + send(to_above, last, "up").astype(F32)
        ).astype(BF16)
        mine = reduce_plane(block, first, second)
        rows.append(mine.reshape(3, 8, width).transpose(1, 0, 2))
    grad_weights = jnp.concatenate(rows, axis=0)
    return (grad_input, grad_weights)


def solution(mesh):
    in_specs = (
        P(("node", "local"), None),
        P(("node", "local"), None),
        P(("node", "local"), None, None),
        P(("node", "local"), None),
    )
    out_specs = (P(("node", "local"), None), P(("node", "local"), None, None))
    return jax.shard_map(body, mesh=mesh, in_specs=in_specs, out_specs=out_specs, check_vma=False)
```

```python
import jax
import jax.numpy as jnp
from jax import lax
from jax.experimental import pallas as pl
from jax.experimental.pallas import tpu as pltpu
from jax.sharding import PartitionSpec as P

AXES = ("node", "local")
X, Y, Z = 0, 1, 2
RING = 4
DEVICES = 128
TILE = 256
BF16 = jnp.bfloat16
F32 = jnp.float32
NT = (((1,), (1,)), ((), ()))
TN = (((0,), (0,)), ((), ()))


def place(device):
    return [device // 64 * 2 + device // 2 % 2, device // 16 % 4, device // 4 % 4, device % 2]


def index(x, y, z, core):
    return (x // 2) * 64 + y * 16 + z * 4 + (x % 2) * 2 + core


def swap(value, axis, wrap):
    pairs = []
    for device in range(DEVICES):
        there = place(device)
        there[axis] = RING - 1 - there[axis] if wrap(there[3]) else there[axis] ^ 1
        pairs.append((device, index(*there)))
    return lax.ppermute(value, AXES, pairs)


def swap_first(value, axis):
    return swap(value, axis, lambda core: core == 1)


def swap_second(value, axis):
    return swap(value, axis, lambda core: core == 0)


def swap_near(value, axis):
    return swap(value, axis, lambda core: False)


def swap_wrap(value, axis):
    return swap(value, axis, lambda core: True)


def swap_core(value):
    return lax.ppermute(value, AXES, [(d, d ^ 1) for d in range(DEVICES)])


def add(a, b):
    return (a.astype(F32) + b.astype(F32)).astype(BF16)


def join(a, b):
    return jnp.concatenate([a, b], axis=1)


def gather(message, axis, last_axis):
    half = join(message, swap_first(message, axis))
    line = join(half, swap_second(half, axis))
    near = join(line, swap_first(line, last_axis))
    return near, swap_second(near, last_axis)


def reduce(near, back, axis, last_axis):
    near = add(near, back)
    n = near.shape[1] // 2
    line = add(near[:, :n], swap_first(near[:, n:], last_axis))
    n //= 2
    half = add(line[:, :n], swap_second(line[:, n:], axis))
    n //= 2
    return half[:, :n].astype(F32) + swap_first(half[:, n:], axis).astype(F32)


def grads_kernel(*refs):
    xs, cs, ws = refs[:4], refs[4:8], refs[8:10]
    g0, g1, a_ref, x_all, c_all, gu, down, hid, sems = refs[10:]
    group = xs[0].shape[0]
    units = ws[0].shape[1]
    moves = []

    def move(source, target):
        moves.append(pltpu.make_async_copy(source, target, sems.at[len(moves)]))
        moves[-1].start()

    for p, w in enumerate(ws):
        for m in range(2):
            move(w.at[m], gu.at[pl.ds((2 * p + m) * units, units)])
        move(w.at[2], down.at[pl.ds(p * units, units)])
    for i in range(4):
        move(xs[i], x_all.at[pl.ds(i * group, group)])
        move(cs[i], c_all.at[pl.ds(i * group, group)])
    for copy in moves[:10]:
        copy.wait()
    tokens = 4 * group
    for t in range(tokens // TILE):
        if t * TILE == 2 * group:
            for copy in moves[10:]:
                copy.wait()
        rows = slice(t * TILE, (t + 1) * TILE)
        z = lax.dot_general(gu[...], x_all[rows], NT, preferred_element_type=F32)
        gh = lax.dot_general(down[...], c_all[rows], NT, preferred_element_type=F32)
        for p in range(2):
            gate = z[2 * p * units : (2 * p + 1) * units]
            up = z[(2 * p + 1) * units : (2 * p + 2) * units]
            grad = gh[p * units : (p + 1) * units]
            sg = 1.0 / (1.0 + jnp.exp(-gate))
            silu = gate * sg
            hid[p * units : (p + 1) * units, rows] = (silu * up).astype(BF16)
            slope = sg + silu * (1.0 - sg)
            a_ref[2 * p * units : (2 * p + 1) * units, rows] = (grad * up * slope).astype(BF16)
            a_ref[(2 * p + 1) * units : (2 * p + 2) * units, rows] = (grad * silu).astype(BF16)
    width = x_all.shape[1]
    for n in range(width // TILE):
        cols = slice(n * TILE, (n + 1) * TILE)
        d_gu = jnp.dot(a_ref[...], x_all[:, cols], preferred_element_type=F32).astype(BF16)
        d_down = jnp.dot(hid[...], c_all[:, cols], preferred_element_type=F32).astype(BF16)
        for p, g in enumerate((g0, g1)):
            for m in range(2):
                g[m, :, cols] = d_gu[(2 * p + m) * units : (2 * p + m + 1) * units]
            g[2, :, cols] = d_down[p * units : (p + 1) * units]


def grads(xs, cs, ws):
    group, width = xs[0].shape
    units = ws[0].shape[1]
    tokens = 4 * group
    return pl.pallas_call(
        grads_kernel,
        out_shape=[jax.ShapeDtypeStruct(w.shape, BF16) for w in ws]
        + [jax.ShapeDtypeStruct((4 * units, tokens), BF16)],
        in_specs=[pl.BlockSpec(memory_space=pl.ANY)] * 10,
        out_specs=[pl.BlockSpec(memory_space=pltpu.VMEM)] * 3,
        scratch_shapes=[
            pltpu.VMEM((tokens, width), BF16),
            pltpu.VMEM((tokens, width), BF16),
            pltpu.VMEM((4 * units, width), BF16),
            pltpu.VMEM((2 * units, width), BF16),
            pltpu.VMEM((2 * units, tokens), BF16),
            pltpu.SemaphoreType.DMA((14,)),
        ],
        compiler_params=pltpu.CompilerParams(vmem_limit_bytes=32 * 1024 * 1024),
        cost_estimate=pl.CostEstimate(
            flops=12 * tokens * width * 2 * units,
            bytes_accessed=4 * tokens * width + 24 * units * width + 8 * units * tokens,
            transcendentals=4 * tokens * units,
        ),
    )(*xs, *cs, *ws)


def input_kernel(a0, a1, w0, w1, w2, w3, own_ref, z_ref, pair_ref, w_all, sems):
    units = w0.shape[1]
    moves = []
    for p, w in enumerate((w0, w1, w2, w3)):
        for m in range(2):
            moves.append(
                pltpu.make_async_copy(
                    w.at[m], w_all.at[pl.ds((2 * p + m) * units, units)], sems.at[2 * p + m]
                )
            )
            moves[-1].start()
    for copy in moves:
        copy.wait()
    half = 4 * units
    group = own_ref.shape[0]
    for i in range(4):
        cols = slice(i * group, (i + 1) * group)
        total = lax.dot_general(a0[:, cols], w_all[:half], TN, preferred_element_type=F32)
        total = total + lax.dot_general(a1[:, cols], w_all[half:], TN, preferred_element_type=F32)
        if i == 0:
            own_ref[...] = total
        elif i == 2:
            z_ref[...] = total
        else:
            pair_ref[i // 2] = total.astype(BF16)


def input_parts(a0, a1, ws):
    units, width = ws[0].shape[1:]
    group = a0.shape[1] // 4
    vmem = pl.BlockSpec(memory_space=pltpu.VMEM)
    return pl.pallas_call(
        input_kernel,
        out_shape=[
            jax.ShapeDtypeStruct((group, width), F32),
            jax.ShapeDtypeStruct((group, width), F32),
            jax.ShapeDtypeStruct((2, group, width), BF16),
        ],
        in_specs=[vmem] * 2 + [pl.BlockSpec(memory_space=pl.ANY)] * 4,
        out_specs=[vmem] * 3,
        scratch_shapes=[pltpu.VMEM((8 * units, width), BF16), pltpu.SemaphoreType.DMA((8,))],
        compiler_params=pltpu.CompilerParams(vmem_limit_bytes=32 * 1024 * 1024),
        cost_estimate=pl.CostEstimate(
            flops=64 * units * width * group,
            bytes_accessed=16 * units * width + 64 * units * group + 12 * group * width,
            transcendentals=0,
        ),
    )(a0, a1, *ws)


def body(activations, cotangent, gate_up, down_proj):
    x_z, c_z = swap_near(activations, Z), swap_near(cotangent, Z)
    xs = [activations, swap_core(activations), x_z, swap_core(x_z)]
    cs = [cotangent, swap_core(cotangent), c_z, swap_core(c_z)]

    message = jnp.concatenate([gate_up.transpose(1, 0, 2), down_proj[None]], axis=0)
    j0, r0 = gather(message, Y, X)
    j1, r1 = gather(swap_wrap(message, Z), X, Y)

    g_r0, g_r1, a_r = grads(xs, cs, [r0, r1])
    back0, back1 = swap_second(g_r0, X), swap_second(g_r1, Y)
    g_j0, g_j1, a_j = grads(xs, cs, [j0, j1])

    own, z_part, pair = input_parts(a_r, a_j, [r0, r1, j0, j1])
    got = swap_core(pair)
    mine = own + got[0].astype(F32)
    z_part = (z_part + got[1].astype(F32)).astype(BF16)
    grad_input = (mine + swap_near(z_part, Z).astype(F32)).astype(BF16)

    rows0 = reduce(g_j0, back0, Y, X)
    rows1 = reduce(g_j1, back1, X, Y).astype(BF16)
    grad_weights = (rows0 + swap_wrap(rows1, Z).astype(F32)).transpose(1, 0, 2)
    return (grad_input, grad_weights)


def solution(mesh):
    in_specs = (
        P(("node", "local"), None),
        P(("node", "local"), None),
        P(("node", "local"), None, None),
        P(("node", "local"), None),
    )
    out_specs = (P(("node", "local"), None), P(("node", "local"), None, None))
    return jax.shard_map(body, mesh=mesh, in_specs=in_specs, out_specs=out_specs, check_vma=False)
```

```python
import jax
import jax.numpy as jnp
from jax import lax
from jax.experimental import pallas as pl
from jax.experimental.pallas import tpu as pltpu
from jax.sharding import PartitionSpec as P

AXES = ("node", "local")
X, Y, Z = 0, 1, 2
RING = 4
DEVICES = 128
TILE = 256
BF16 = jnp.bfloat16
F32 = jnp.float32
NT = (((1,), (1,)), ((), ()))
TN = (((0,), (0,)), ((), ()))


def place(device):
    return [device // 64 * 2 + device // 2 % 2, device // 16 % 4, device // 4 % 4, device % 2]


def index(x, y, z, core):
    return (x // 2) * 64 + y * 16 + z * 4 + (x % 2) * 2 + core


def swap(value, axis, wrap):
    pairs = []
    for device in range(DEVICES):
        there = place(device)
        there[axis] = RING - 1 - there[axis] if wrap(there[3]) else there[axis] ^ 1
        pairs.append((device, index(*there)))
    return lax.ppermute(value, AXES, pairs)


def swap_first(value, axis):
    return swap(value, axis, lambda core: core == 1)


def swap_second(value, axis):
    return swap(value, axis, lambda core: core == 0)


def swap_near(value, axis):
    return swap(value, axis, lambda core: False)


def swap_wrap(value, axis):
    return swap(value, axis, lambda core: True)


def swap_over(value, axis):
    pairs = []
    for device in range(DEVICES):
        there = place(device)
        there[axis] = RING - 1 - there[axis] if there[3] == 1 else there[axis] ^ 1
        there[Z] = RING - 1 - there[Z]
        pairs.append((device, index(*there)))
    return lax.ppermute(value, AXES, pairs)


def swap_core(value):
    return lax.ppermute(value, AXES, [(d, d ^ 1) for d in range(DEVICES)])


def add(a, b):
    return (a.astype(F32) + b.astype(F32)).astype(BF16)


def join(a, b):
    return jnp.concatenate([a, b], axis=1)


def gather(half, swaps):
    for swap_with in swaps[:-1]:
        half = join(half, swap_with(half))
    return half, swaps[-1](half)


def reduce(near, back, swaps):
    near = add(near, back)
    for swap_with in swaps[-2::-1]:
        n = near.shape[1] // 2
        near = add(near[:, :n], swap_with(near[:, n:]))
    return near


def rows_of(refs, start, stop, cols=slice(None)):
    parts = []
    for ref in refs:
        n = ref.shape[0]
        if start < n and stop > 0:
            parts.append(ref[max(start, 0) : min(stop, n), cols])
        start, stop = start - n, stop - n
    return parts[0] if len(parts) == 1 else jnp.concatenate(parts, axis=0)


def grads_kernel(n, *refs):
    xs, cs, ws = refs[:n], refs[n : 2 * n], refs[2 * n : 2 * n + 2]
    g0, g1, a_ref, hid = refs[2 * n + 2 :]
    units, width = ws[0].shape[1:]
    gu = jnp.concatenate([w[m] for w in ws for m in range(2)], axis=0)
    down = jnp.concatenate([w[2] for w in ws], axis=0)
    tokens = hid.shape[1]
    for t in range(tokens // TILE):
        rows = slice(t * TILE, (t + 1) * TILE)
        x = rows_of(xs, t * TILE, (t + 1) * TILE)
        c = rows_of(cs, t * TILE, (t + 1) * TILE)
        z = lax.dot_general(gu, x, NT, preferred_element_type=F32)
        gh = lax.dot_general(down, c, NT, preferred_element_type=F32)
        for p in range(2):
            gate = z[2 * p * units : (2 * p + 1) * units]
            up = z[(2 * p + 1) * units : (2 * p + 2) * units]
            grad = gh[p * units : (p + 1) * units]
            sg = 1.0 / (1.0 + jnp.exp(-gate))
            silu = gate * sg
            hid[p * units : (p + 1) * units, rows] = (silu * up).astype(BF16)
            slope = sg + silu * (1.0 - sg)
            a_ref[2 * p * units : (2 * p + 1) * units, rows] = (grad * up * slope).astype(BF16)
            a_ref[(2 * p + 1) * units : (2 * p + 2) * units, rows] = (grad * silu).astype(BF16)
    for k in range(width // TILE):
        cols = slice(k * TILE, (k + 1) * TILE)
        x = rows_of(xs, 0, tokens, cols)
        c = rows_of(cs, 0, tokens, cols)
        d_gu = jnp.dot(a_ref[...], x, preferred_element_type=F32).astype(BF16)
        d_down = jnp.dot(hid[...], c, preferred_element_type=F32).astype(BF16)
        for p, g in enumerate((g0, g1)):
            for m in range(2):
                g[m, :, cols] = d_gu[(2 * p + m) * units : (2 * p + m + 1) * units]
            g[2, :, cols] = d_down[p * units : (p + 1) * units]


def grads(xs, cs, ws):
    units, width = ws[0].shape[1:]
    tokens = sum(x.shape[0] for x in xs)
    vmem = pl.BlockSpec(memory_space=pltpu.VMEM)

    def kernel(*refs):
        grads_kernel(len(xs), *refs)

    return pl.pallas_call(
        kernel,
        out_shape=[jax.ShapeDtypeStruct(w.shape, BF16) for w in ws]
        + [jax.ShapeDtypeStruct((4 * units, tokens), BF16)],
        in_specs=[vmem] * (2 * len(xs) + 2),
        out_specs=[vmem] * 3,
        scratch_shapes=[pltpu.VMEM((2 * units, tokens), BF16)],
        compiler_params=pltpu.CompilerParams(vmem_limit_bytes=32 * 1024 * 1024),
        cost_estimate=pl.CostEstimate(
            flops=12 * tokens * width * 2 * units,
            bytes_accessed=4 * tokens * width + 24 * units * width + 8 * units * tokens,
            transcendentals=4 * tokens * units,
        ),
    )(*xs, *cs, *ws)


def input_kernel(a0, a1, w0, w1, w2, w3, own_ref, z_ref, pair_ref):
    w_all = jnp.concatenate([w[m] for w in (w0, w1, w2, w3) for m in range(2)], axis=0)
    group = own_ref.shape[0]
    for i in range(4):
        cols = slice(i * group, (i + 1) * group)
        a = jnp.concatenate([a0[:, cols], a1[:, cols]], axis=0)
        total = lax.dot_general(a, w_all, TN, preferred_element_type=F32)
        if i == 0:
            own_ref[...] = total
        elif i == 2:
            z_ref[...] = total
        else:
            pair_ref[i // 2] = total.astype(BF16)


def input_parts(a0, a1, ws):
    units, width = ws[0].shape[1:]
    group = a0.shape[1] // 4
    vmem = pl.BlockSpec(memory_space=pltpu.VMEM)
    return pl.pallas_call(
        input_kernel,
        out_shape=[
            jax.ShapeDtypeStruct((group, width), F32),
            jax.ShapeDtypeStruct((group, width), F32),
            jax.ShapeDtypeStruct((2, group, width), BF16),
        ],
        in_specs=[vmem] * 6,
        out_specs=[vmem] * 3,
        compiler_params=pltpu.CompilerParams(vmem_limit_bytes=32 * 1024 * 1024),
        cost_estimate=pl.CostEstimate(
            flops=64 * units * width * group,
            bytes_accessed=16 * units * width + 64 * units * group + 12 * group * width,
            transcendentals=0,
        ),
    )(a0, a1, *ws)


def body(activations, cotangent, gate_up, down_proj):
    message = jnp.concatenate([gate_up.transpose(1, 0, 2), down_proj[None]], axis=0)
    swaps0 = [lambda v: swap_second(v, Y), lambda v: swap_first(v, X), lambda v: swap_second(v, X)]
    swaps1 = [lambda v: swap_second(v, X), lambda v: swap_first(v, Y), lambda v: swap_second(v, Y)]

    n = activations.shape[0] // 2
    x_a = swap_near(activations[:n], Z)
    half0 = join(message, swap_first(message, Y))
    half1 = join(swap_wrap(message, Z), swap_over(message, X))
    x_core, c_core = swap_core(activations), swap_core(cotangent)

    half0, half1, x_a = lax.optimization_barrier((half0, half1, x_a))
    x_b = swap_near(activations[n:], Z)
    line0 = join(half0, swaps0[0](half0))
    line1 = join(half1, swaps1[0](half1))
    line0, line1, x_b = lax.optimization_barrier((line0, line1, x_b))
    x_z = jnp.concatenate([x_a, x_b], axis=0)
    x_zc = swap_core(x_z)
    c_a = swap_near(cotangent[:n], Z)
    j0 = join(line0, swaps0[1](line0))
    j1 = join(line1, swaps1[1](line1))
    j0, j1, c_a = lax.optimization_barrier((j0, j1, c_a))
    c_b = swap_near(cotangent[n:], Z)
    r0, r1 = swaps0[2](j0), swaps1[2](j1)
    c_z = jnp.concatenate([c_a, c_b], axis=0)
    xs = [activations, x_core, x_z, x_zc]
    cs = [cotangent, c_core, c_z, swap_core(c_z)]

    g_r0, g_r1, a_r = grads(xs, cs, [r0, r1])
    back0, back1 = swaps0[2](g_r0), swaps1[2](g_r1)
    g_j0, g_j1, a_j = grads(xs, cs, [j0, j1])

    own, z_part, pair = input_parts(a_r, a_j, [r0, r1, j0, j1])
    got = swap_core(pair)
    mine = own + got[0].astype(F32)
    z_part = (z_part + got[1].astype(F32)).astype(BF16)
    grad_input = (mine + swap_near(z_part, Z).astype(F32)).astype(BF16)

    half0 = reduce(g_j0, back0, swaps0)
    half1 = reduce(g_j1, back1, swaps1)
    n = half0.shape[1] // 2
    total = half0[:, :n].astype(F32) + swap_first(half0[:, n:], Y).astype(F32)
    total = total + swap_wrap(half1[:, :n], Z).astype(F32) + swap_over(half1[:, n:], X).astype(F32)
    return (grad_input, total.transpose(1, 0, 2))


def solution(mesh):
    in_specs = (
        P(("node", "local"), None),
        P(("node", "local"), None),
        P(("node", "local"), None, None),
        P(("node", "local"), None),
    )
    out_specs = (P(("node", "local"), None), P(("node", "local"), None, None))
    return jax.shard_map(body, mesh=mesh, in_specs=in_specs, out_specs=out_specs, check_vma=False)
```

```python
import jax
import jax.numpy as jnp
from jax import lax
from jax.experimental import pallas as pl
from jax.experimental.pallas import tpu as pltpu
from jax.sharding import PartitionSpec as P

AXES = ("x_hi", "y", "z", "x_lo", "core")
SIZES = (2, 4, 4, 2, 2)
X, Y, Z = 0, 1, 2
RING = 4
DEVICES = 128
TILE = 256
BF16 = jnp.bfloat16
F32 = jnp.float32
NT = (((1,), (1,)), ((), ()))
TN = (((0,), (0,)), ((), ()))


def place(device):
    return [device // 64 * 2 + device // 2 % 2, device // 16 % 4, device // 4 % 4, device % 2]


def index(x, y, z, core):
    return (x // 2) * 64 + y * 16 + z * 4 + (x % 2) * 2 + core


def swap(value, axis, wrap):
    pairs = []
    for device in range(DEVICES):
        there = place(device)
        there[axis] = RING - 1 - there[axis] if wrap(there[3]) else there[axis] ^ 1
        pairs.append((device, index(*there)))
    return lax.ppermute(value, AXES, pairs)


def swap_first(value, axis):
    return swap(value, axis, lambda core: core == 1)


def swap_second(value, axis):
    return swap(value, axis, lambda core: core == 0)


def swap_near(value, axis):
    return swap(value, axis, lambda core: False)


def swap_wrap(value, axis):
    return swap(value, axis, lambda core: True)


def swap_over(value, axis):
    pairs = []
    for device in range(DEVICES):
        there = place(device)
        there[axis] = RING - 1 - there[axis] if there[3] == 1 else there[axis] ^ 1
        there[Z] = RING - 1 - there[Z]
        pairs.append((device, index(*there)))
    return lax.ppermute(value, AXES, pairs)


def swap_core(value):
    return lax.ppermute(value, AXES, [(d, d ^ 1) for d in range(DEVICES)])


def add(a, b):
    return (a.astype(F32) + b.astype(F32)).astype(BF16)


def join(a, b):
    return jnp.concatenate([a, b], axis=1)


def rows_of(refs, start, stop, cols=slice(None)):
    parts = []
    for ref in refs:
        n = ref.shape[0]
        if start < n and stop > 0:
            parts.append(ref[max(start, 0) : min(stop, n), cols])
        start, stop = start - n, stop - n
    return parts[0] if len(parts) == 1 else jnp.concatenate(parts, axis=0)


def grads_kernel(n, *refs):
    xs, cs, w = refs[:n], refs[n : 2 * n], refs[2 * n]
    g, a_ref, hid = refs[2 * n + 1 :]
    units, width = w.shape[1:]
    gu = w[:2].reshape(2 * units, width)
    tokens = hid.shape[1]
    for t in range(tokens // TILE):
        rows = slice(t * TILE, (t + 1) * TILE)
        x = rows_of(xs, t * TILE, (t + 1) * TILE)
        c = rows_of(cs, t * TILE, (t + 1) * TILE)
        z = lax.dot_general(gu, x, NT, preferred_element_type=F32)
        grad = lax.dot_general(w[2], c, NT, preferred_element_type=F32)
        gate, up = z[:units], z[units:]
        sg = 1.0 / (1.0 + jnp.exp(-gate))
        silu = gate * sg
        hid[:, rows] = (silu * up).astype(BF16)
        slope = sg + silu * (1.0 - sg)
        a_ref[:units, rows] = (grad * up * slope).astype(BF16)
        a_ref[units:, rows] = (grad * silu).astype(BF16)
    for k in range(width // TILE):
        cols = slice(k * TILE, (k + 1) * TILE)
        x = rows_of(xs, 0, tokens, cols)
        c = rows_of(cs, 0, tokens, cols)
        d_gu = jnp.dot(a_ref[...], x, preferred_element_type=F32).astype(BF16)
        g[0, :, cols] = d_gu[:units]
        g[1, :, cols] = d_gu[units:]
        g[2, :, cols] = jnp.dot(hid[...], c, preferred_element_type=F32).astype(BF16)


def grads(xs, cs, w):
    units, width = w.shape[1:]
    tokens = sum(x.shape[0] for x in xs)
    vmem = pl.BlockSpec(memory_space=pltpu.VMEM)

    def kernel(*refs):
        grads_kernel(len(xs), *refs)

    return pl.pallas_call(
        kernel,
        out_shape=[
            jax.ShapeDtypeStruct(w.shape, BF16),
            jax.ShapeDtypeStruct((2 * units, tokens), BF16),
        ],
        in_specs=[vmem] * (2 * len(xs) + 1),
        out_specs=[vmem] * 2,
        scratch_shapes=[pltpu.VMEM((units, tokens), BF16)],
        compiler_params=pltpu.CompilerParams(vmem_limit_bytes=32 * 1024 * 1024),
        cost_estimate=pl.CostEstimate(
            flops=12 * tokens * width * units,
            bytes_accessed=4 * tokens * width + 12 * units * width + 4 * units * tokens,
            transcendentals=2 * tokens * units,
        ),
    )(*xs, *cs, w)


def input_kernel(a0, a1, w0, w1, own_ref, z_ref, pair_ref):
    w_all = jnp.concatenate([w[m] for w in (w0, w1) for m in range(2)], axis=0)
    group = own_ref.shape[0]
    for i in range(4):
        cols = slice(i * group, (i + 1) * group)
        a = jnp.concatenate([a0[:, cols], a1[:, cols]], axis=0)
        total = lax.dot_general(a, w_all, TN, preferred_element_type=F32)
        if i == 0:
            own_ref[...] = total
        elif i == 2:
            z_ref[...] = total
        else:
            pair_ref[i // 2] = total.astype(BF16)


def input_parts(a0, a1, ws):
    units, width = ws[0].shape[1:]
    group = a0.shape[1] // 4
    vmem = pl.BlockSpec(memory_space=pltpu.VMEM)
    return pl.pallas_call(
        input_kernel,
        out_shape=[
            jax.ShapeDtypeStruct((group, width), F32),
            jax.ShapeDtypeStruct((group, width), F32),
            jax.ShapeDtypeStruct((2, group, width), BF16),
        ],
        in_specs=[vmem] * 4,
        out_specs=[vmem] * 3,
        compiler_params=pltpu.CompilerParams(vmem_limit_bytes=32 * 1024 * 1024),
        cost_estimate=pl.CostEstimate(
            flops=32 * units * width * group,
            bytes_accessed=8 * units * width + 32 * units * group + 12 * group * width,
            transcendentals=0,
        ),
    )(a0, a1, *ws)


def gather(value, axis):
    return lax.all_gather(value, axis, axis=1, tiled=True)


def scatter(value, axis):
    return lax.psum_scatter(value, axis, scatter_dimension=1, tiled=True)


def body(activations, cotangent, gate_up, down_proj):
    message = jnp.concatenate([gate_up.transpose(1, 0, 2), down_proj[None]], axis=0)
    across = ("x_hi", "x_lo")
    x_z = swap_near(activations, Z)
    w0 = gather(message, "y")
    w1 = gather(swap_wrap(message, Z), across)
    x_core, c_core = swap_core(activations), swap_core(cotangent)
    w0, w1, x_z, c_own = lax.optimization_barrier((w0, w1, x_z, cotangent))
    c_z = swap_near(c_own, Z)
    w0 = gather(w0, across)
    w1 = gather(w1, "y")
    xs = [activations, x_core, x_z, swap_core(x_z)]
    cs = [cotangent, c_core, c_z, swap_core(c_z)]

    g0, a0 = grads(xs, cs, w0)
    half0 = scatter(g0, across)
    g1, a1 = grads(xs, cs, w1)
    half1 = scatter(g1, "y")

    own, z_part, pair = input_parts(a0, a1, [w0, w1])
    got = swap_core(pair)
    mine = own + got[0].astype(F32)
    z_part = (z_part + got[1].astype(F32)).astype(BF16)
    grad_input = (mine + swap_near(z_part, Z).astype(F32)).astype(BF16)

    total0 = scatter(half0, "y")
    total1 = swap_wrap(scatter(half1, across), Z)
    total = total0.astype(F32) + total1.astype(F32)
    return (grad_input, total.transpose(1, 0, 2))


def solution(mesh):
    split = jax.sharding.Mesh(mesh.devices.reshape(SIZES), AXES)
    rows = P(AXES, None)
    rows3 = P(AXES, None, None)
    return jax.shard_map(
        body, mesh=split, in_specs=(rows, rows, rows3, rows), out_specs=(rows, rows3), check_vma=False
    )
```

```python
import jax
import jax.numpy as jnp
from jax import lax
from jax.experimental import pallas as pl
from jax.experimental.pallas import tpu as pltpu
from jax.sharding import PartitionSpec as P

AXES = ("node", "local")
X, Y, Z = 0, 1, 2
RING = 4
DEVICES = 128
TILE = 256
BF16 = jnp.bfloat16
F32 = jnp.float32
NT = (((1,), (1,)), ((), ()))
TN = (((0,), (0,)), ((), ()))


def place(device):
    return [device // 64 * 2 + device // 2 % 2, device // 16 % 4, device // 4 % 4, device % 2]


def index(x, y, z, core):
    return (x // 2) * 64 + y * 16 + z * 4 + (x % 2) * 2 + core


def swap(value, axis, wrap):
    pairs = []
    for device in range(DEVICES):
        there = place(device)
        there[axis] = RING - 1 - there[axis] if wrap(there[3]) else there[axis] ^ 1
        pairs.append((device, index(*there)))
    return lax.ppermute(value, AXES, pairs)


def swap_first(value, axis):
    return swap(value, axis, lambda core: core == 1)


def swap_second(value, axis):
    return swap(value, axis, lambda core: core == 0)


def swap_near(value, axis):
    return swap(value, axis, lambda core: False)


def swap_wrap(value, axis):
    return swap(value, axis, lambda core: True)


def swap_corner(value):
    pairs = []
    for device in range(DEVICES):
        there = place(device)
        for axis in (X, Y):
            there[axis] = RING - 1 - there[axis] if there[3] == 1 else there[axis] ^ 1
        pairs.append((device, index(*there)))
    return lax.ppermute(value, AXES, pairs)


def swap_core(value):
    return lax.ppermute(value, AXES, [(d, d ^ 1) for d in range(DEVICES)])


def add(a, b):
    return (a.astype(F32) + b.astype(F32)).astype(BF16)


def join(*blocks):
    return jnp.concatenate(blocks, axis=1)


def gather_block(message):
    return join(message, swap_first(message, Y), swap_first(message, X), swap_corner(message))


def reduce_block(block):
    n = block.shape[1] // 4
    own, along_y, along_x, corner = (block[:, i * n : (i + 1) * n] for i in range(4))
    total = own.astype(F32) + swap_first(along_y, Y).astype(F32)
    return total + swap_first(along_x, X).astype(F32) + swap_corner(corner).astype(F32)


def halve(both, axis):
    n = both.shape[1] // 2
    return add(both[:, :n], swap_second(both[:, n:], axis))


def rows_of(refs, start, stop, cols=slice(None)):
    parts = []
    for ref in refs:
        n = ref.shape[0]
        if start < n and stop > 0:
            parts.append(ref[max(start, 0) : min(stop, n), cols])
        start, stop = start - n, stop - n
    return parts[0] if len(parts) == 1 else jnp.concatenate(parts, axis=0)


def grads_kernel(n, *refs):
    xs, cs, refs = refs[:n], refs[n : 2 * n], refs[2 * n :]
    a_ref, hid = refs[-2:]
    parts = len(refs) // 2 - 1
    ws, gs = refs[:parts], refs[parts:-2]
    units, width = ws[0].shape[1:]
    gu = jnp.concatenate([w[m] for w in ws for m in range(2)], axis=0)
    down = jnp.concatenate([w[2] for w in ws], axis=0)
    tokens = hid.shape[1]
    for t in range(tokens // TILE):
        rows = slice(t * TILE, (t + 1) * TILE)
        x = rows_of(xs, t * TILE, (t + 1) * TILE)
        c = rows_of(cs, t * TILE, (t + 1) * TILE)
        z = lax.dot_general(gu, x, NT, preferred_element_type=F32)
        gh = lax.dot_general(down, c, NT, preferred_element_type=F32)
        for p in range(parts):
            gate = z[2 * p * units : (2 * p + 1) * units]
            up = z[(2 * p + 1) * units : (2 * p + 2) * units]
            grad = gh[p * units : (p + 1) * units]
            sg = 1.0 / (1.0 + jnp.exp(-gate))
            silu = gate * sg
            hid[p * units : (p + 1) * units, rows] = (silu * up).astype(BF16)
            slope = sg + silu * (1.0 - sg)
            a_ref[2 * p * units : (2 * p + 1) * units, rows] = (grad * up * slope).astype(BF16)
            a_ref[(2 * p + 1) * units : (2 * p + 2) * units, rows] = (grad * silu).astype(BF16)
    for k in range(width // TILE):
        cols = slice(k * TILE, (k + 1) * TILE)
        x = rows_of(xs, 0, tokens, cols)
        c = rows_of(cs, 0, tokens, cols)
        d_gu = jnp.dot(a_ref[...], x, preferred_element_type=F32).astype(BF16)
        d_down = jnp.dot(hid[...], c, preferred_element_type=F32).astype(BF16)
        for p, g in enumerate(gs):
            for m in range(2):
                g[m, :, cols] = d_gu[(2 * p + m) * units : (2 * p + m + 1) * units]
            g[2, :, cols] = d_down[p * units : (p + 1) * units]


def grads(xs, cs, ws):
    units, width = ws[0].shape[1:]
    tokens = sum(x.shape[0] for x in xs)
    vmem = pl.BlockSpec(memory_space=pltpu.VMEM)

    def kernel(*refs):
        grads_kernel(len(xs), *refs)

    return pl.pallas_call(
        kernel,
        out_shape=[jax.ShapeDtypeStruct(w.shape, BF16) for w in ws]
        + [jax.ShapeDtypeStruct((2 * len(ws) * units, tokens), BF16)],
        in_specs=[vmem] * (2 * len(xs) + len(ws)),
        out_specs=[vmem] * (len(ws) + 1),
        scratch_shapes=[pltpu.VMEM((len(ws) * units, tokens), BF16)],
        compiler_params=pltpu.CompilerParams(vmem_limit_bytes=32 * 1024 * 1024),
        cost_estimate=pl.CostEstimate(
            flops=width, bytes_accessed=width, transcendentals=0
        ),
    )(*xs, *cs, *ws)


def input_kernel(n, *refs):
    parts, ws = refs[:n], refs[n:-3]
    own_ref, z_ref, pair_ref = refs[-3:]
    w_all = jnp.concatenate([w[m] for w in ws for m in range(2)], axis=0)
    group = own_ref.shape[0]
    for i in range(4):
        cols = slice(i * group, (i + 1) * group)
        a = jnp.concatenate([part[:, cols] for part in parts], axis=0)
        total = lax.dot_general(a, w_all, TN, preferred_element_type=F32)
        if i == 0:
            own_ref[...] = total
        elif i == 2:
            z_ref[...] = total
        else:
            pair_ref[i // 2] = total.astype(BF16)


def input_parts(parts, ws):
    units, width = ws[0].shape[1:]
    group = parts[0].shape[1] // 4
    vmem = pl.BlockSpec(memory_space=pltpu.VMEM)

    def kernel(*refs):
        input_kernel(len(parts), *refs)

    return pl.pallas_call(
        kernel,
        out_shape=[
            jax.ShapeDtypeStruct((group, width), F32),
            jax.ShapeDtypeStruct((group, width), F32),
            jax.ShapeDtypeStruct((2, group, width), BF16),
        ],
        in_specs=[vmem] * (len(parts) + len(ws)),
        out_specs=[vmem] * 3,
        compiler_params=pltpu.CompilerParams(vmem_limit_bytes=32 * 1024 * 1024),
        cost_estimate=pl.CostEstimate(
            flops=width, bytes_accessed=width, transcendentals=0
        ),
    )(*parts, *ws)


def body(activations, cotangent, gate_up, down_proj):
    x_z = swap_near(activations, Z)
    message = jnp.concatenate([gate_up.transpose(1, 0, 2), down_proj[None]], axis=0)
    other = swap_wrap(message, Z)
    block0 = gather_block(message)
    block1 = gather_block(other)
    block1, x_z, c_own = lax.optimization_barrier((block1, x_z, cotangent))
    c_z = swap_near(c_own, Z)
    j0 = join(block0, swap_second(block0, Y))
    j1 = join(block1, swap_second(block1, X))
    r0, r1 = swap_second(j0, X), swap_second(j1, Y)
    xs = [activations, swap_core(activations), x_z, swap_core(x_z)]
    cs = [cotangent, swap_core(cotangent), c_z, swap_core(c_z)]

    g_r0, a_r0 = grads(xs, cs, [r0])
    back0 = swap_second(g_r0, X)
    g_r1, a_r1 = grads(xs, cs, [r1])
    back1 = swap_second(g_r1, Y)
    j0, j1, a_r1 = lax.optimization_barrier((j0, j1, a_r1))
    g_j0, g_j1, a_j = grads(xs, cs, [j0, j1])

    own, z_part, pair = input_parts([a_r0, a_r1, a_j], [r0, r1, j0, j1])
    got = swap_core(pair)
    near0, near1 = add(g_j0, back0), add(g_j1, back1)
    near0, near1, z_part = lax.optimization_barrier((near0, near1, z_part))
    mine = own + got[0].astype(F32)
    z_part = swap_near((z_part + got[1].astype(F32)).astype(BF16), Z)

    total1 = reduce_block(halve(near1, X)).astype(BF16)
    total1, z_part = lax.optimization_barrier((total1, z_part))
    grad_input = (mine + z_part.astype(F32)).astype(BF16)
    total0 = reduce_block(halve(near0, Y))
    total = total0 + swap_wrap(total1, Z).astype(F32)
    return (grad_input, total.transpose(1, 0, 2))


def solution(mesh):
    in_specs = (
        P(("node", "local"), None),
        P(("node", "local"), None),
        P(("node", "local"), None, None),
        P(("node", "local"), None),
    )
    out_specs = (P(("node", "local"), None), P(("node", "local"), None, None))
    return jax.shard_map(body, mesh=mesh, in_specs=in_specs, out_specs=out_specs, check_vma=False)
```

```python
import jax
import jax.numpy as jnp
from jax import lax
from jax.experimental import pallas as pl
from jax.experimental.pallas import tpu as pltpu
from jax.sharding import PartitionSpec as P

AXES = ("node", "local")
X, Y, Z = 0, 1, 2
RING = 4
DEVICES = 128
TILE = 256
BF16 = jnp.bfloat16
F32 = jnp.float32
NT = (((1,), (1,)), ((), ()))
TN = (((0,), (0,)), ((), ()))


def place(device):
    return [device // 64 * 2 + device // 2 % 2, device // 16 % 4, device // 4 % 4, device % 2]


def index(x, y, z, core):
    return (x // 2) * 64 + y * 16 + z * 4 + (x % 2) * 2 + core


def swap(value, axis, wrap):
    pairs = []
    for device in range(DEVICES):
        there = place(device)
        there[axis] = RING - 1 - there[axis] if wrap(there[3]) else there[axis] ^ 1
        pairs.append((device, index(*there)))
    return lax.ppermute(value, AXES, pairs)


def swap_first(value, axis):
    return swap(value, axis, lambda core: core == 1)


def swap_second(value, axis):
    return swap(value, axis, lambda core: core == 0)


def swap_near(value, axis):
    return swap(value, axis, lambda core: False)


def swap_wrap(value, axis):
    return swap(value, axis, lambda core: True)


def swap_corner(value):
    pairs = []
    for device in range(DEVICES):
        there = place(device)
        for axis in (X, Y):
            there[axis] = RING - 1 - there[axis] if there[3] == 1 else there[axis] ^ 1
        pairs.append((device, index(*there)))
    return lax.ppermute(value, AXES, pairs)


def swap_core(value):
    return lax.ppermute(value, AXES, [(d, d ^ 1) for d in range(DEVICES)])


def add(a, b):
    return (a.astype(F32) + b.astype(F32)).astype(BF16)


def join(*blocks):
    return jnp.concatenate(blocks, axis=1)


def gather_block(message):
    return join(message, swap_first(message, Y), swap_first(message, X), swap_corner(message))


def reduce_block(block):
    n = block.shape[1] // 4
    own, along_y, along_x, corner = (block[:, i * n : (i + 1) * n] for i in range(4))
    total = own.astype(F32) + swap_first(along_y, Y).astype(F32)
    return total + swap_first(along_x, X).astype(F32) + swap_corner(corner).astype(F32)


def reduce(near, back, axis):
    n = near.shape[1] // 2
    got = swap_second(add(near[:, n:], back[:, n:]), axis)
    return (near[:, :n].astype(F32) + back[:, :n].astype(F32) + got.astype(F32)).astype(BF16)


def rows_of(refs, start, stop, cols=slice(None)):
    parts = []
    for ref in refs:
        n = ref.shape[0]
        if start < n and stop > 0:
            parts.append(ref[max(start, 0) : min(stop, n), cols])
        start, stop = start - n, stop - n
    return parts[0] if len(parts) == 1 else jnp.concatenate(parts, axis=0)


def grads_kernel(n, *refs):
    xs, cs, refs = refs[:n], refs[n : 2 * n], refs[2 * n :]
    a_ref, hid = refs[-2:]
    parts = len(refs) // 2 - 1
    ws, gs = refs[:parts], refs[parts:-2]
    units, width = ws[0].shape[1:]
    gu = jnp.concatenate([w[m] for w in ws for m in range(2)], axis=0)
    down = jnp.concatenate([w[2] for w in ws], axis=0)
    tokens = hid.shape[1]
    for t in range(tokens // TILE):
        rows = slice(t * TILE, (t + 1) * TILE)
        x = rows_of(xs, t * TILE, (t + 1) * TILE)
        c = rows_of(cs, t * TILE, (t + 1) * TILE)
        z = lax.dot_general(gu, x, NT, preferred_element_type=F32)
        gh = lax.dot_general(down, c, NT, preferred_element_type=F32)
        for p in range(parts):
            gate = z[2 * p * units : (2 * p + 1) * units]
            up = z[(2 * p + 1) * units : (2 * p + 2) * units]
            grad = gh[p * units : (p + 1) * units]
            sg = 1.0 / (1.0 + jnp.exp(-gate))
            silu = gate * sg
            hid[p * units : (p + 1) * units, rows] = (silu * up).astype(BF16)
            slope = sg + silu * (1.0 - sg)
            a_ref[2 * p * units : (2 * p + 1) * units, rows] = (grad * up * slope).astype(BF16)
            a_ref[(2 * p + 1) * units : (2 * p + 2) * units, rows] = (grad * silu).astype(BF16)
    for k in range(width // TILE):
        cols = slice(k * TILE, (k + 1) * TILE)
        x = rows_of(xs, 0, tokens, cols)
        c = rows_of(cs, 0, tokens, cols)
        d_gu = jnp.dot(a_ref[...], x, preferred_element_type=F32).astype(BF16)
        d_down = jnp.dot(hid[...], c, preferred_element_type=F32).astype(BF16)
        for p, g in enumerate(gs):
            for m in range(2):
                g[m, :, cols] = d_gu[(2 * p + m) * units : (2 * p + m + 1) * units]
            g[2, :, cols] = d_down[p * units : (p + 1) * units]


def grads(xs, cs, ws):
    units, width = ws[0].shape[1:]
    tokens = sum(x.shape[0] for x in xs)
    vmem = pl.BlockSpec(memory_space=pltpu.VMEM)

    def kernel(*refs):
        grads_kernel(len(xs), *refs)

    return pl.pallas_call(
        kernel,
        out_shape=[jax.ShapeDtypeStruct(w.shape, BF16) for w in ws]
        + [jax.ShapeDtypeStruct((2 * len(ws) * units, tokens), BF16)],
        in_specs=[vmem] * (2 * len(xs) + len(ws)),
        out_specs=[vmem] * (len(ws) + 1),
        scratch_shapes=[pltpu.VMEM((len(ws) * units, tokens), BF16)],
        compiler_params=pltpu.CompilerParams(vmem_limit_bytes=32 * 1024 * 1024),
        cost_estimate=pl.CostEstimate(
            flops=width, bytes_accessed=width, transcendentals=0
        ),
    )(*xs, *cs, *ws)


def input_kernel(n, *refs):
    parts, ws = refs[:n], refs[n:-3]
    own_ref, z_ref, pair_ref = refs[-3:]
    w_all = jnp.concatenate([w[m] for w in ws for m in range(2)], axis=0)
    group = own_ref.shape[0]
    for i in range(4):
        cols = slice(i * group, (i + 1) * group)
        a = jnp.concatenate([part[:, cols] for part in parts], axis=0)
        total = lax.dot_general(a, w_all, TN, preferred_element_type=F32)
        if i == 0:
            own_ref[...] = total
        elif i == 2:
            z_ref[...] = total
        else:
            pair_ref[i // 2] = total.astype(BF16)


def input_parts(parts, ws):
    units, width = ws[0].shape[1:]
    group = parts[0].shape[1] // 4
    vmem = pl.BlockSpec(memory_space=pltpu.VMEM)

    def kernel(*refs):
        input_kernel(len(parts), *refs)

    return pl.pallas_call(
        kernel,
        out_shape=[
            jax.ShapeDtypeStruct((group, width), F32),
            jax.ShapeDtypeStruct((group, width), F32),
            jax.ShapeDtypeStruct((2, group, width), BF16),
        ],
        in_specs=[vmem] * (len(parts) + len(ws)),
        out_specs=[vmem] * 3,
        compiler_params=pltpu.CompilerParams(vmem_limit_bytes=32 * 1024 * 1024),
        cost_estimate=pl.CostEstimate(
            flops=width, bytes_accessed=width, transcendentals=0
        ),
    )(*parts, *ws)


def body(activations, cotangent, gate_up, down_proj):
    x_z = swap_near(activations, Z)
    message = jnp.concatenate([gate_up.transpose(1, 0, 2), down_proj[None]], axis=0)
    message = lax.optimization_barrier(message)
    block1 = gather_block(swap_wrap(message, Z))
    block0 = gather_block(message)
    block1, x_z, c_own = lax.optimization_barrier((block1, x_z, cotangent))
    c_z = swap_near(c_own, Z)
    j0 = join(block0, swap_second(block0, Y))
    j1 = join(block1, swap_second(block1, X))
    r0, r1 = swap_second(j0, X), swap_second(j1, Y)
    xs = [activations, swap_core(activations), x_z, swap_core(x_z)]
    cs = [cotangent, swap_core(cotangent), c_z, swap_core(c_z)]

    g_j0, a_j0 = grads(xs, cs, [j0])
    r0, r1, a_j0 = lax.optimization_barrier((r0, r1, a_j0))
    g_r1, a_r1 = grads(xs, cs, [r1])
    back1 = swap_second(g_r1, Y)
    r0, a_r1 = lax.optimization_barrier((r0, a_r1))
    g_r0, a_r0 = grads(xs, cs, [r0])
    back0 = swap_second(g_r0, X)
    j1, a_r0 = lax.optimization_barrier((j1, a_r0))
    g_j1, a_j1 = grads(xs, cs, [j1])

    own, z_part, pair = input_parts([a_r0, a_r1, a_j0, a_j1], [r0, r1, j0, j1])
    got = swap_core(pair)
    back0, back1, z_part = lax.optimization_barrier((back0, back1, z_part))
    mine = own + got[0].astype(F32)
    z_part = swap_near((z_part + got[1].astype(F32)).astype(BF16), Z)
    total1 = reduce_block(reduce(g_j1, back1, X)).astype(BF16)
    total0 = reduce_block(reduce(g_j0, back0, Y))
    grad_input = (mine + z_part.astype(F32)).astype(BF16)
    total0, grad_input = lax.optimization_barrier((total0, grad_input))
    total = total0 + swap_wrap(total1, Z).astype(F32)
    return (grad_input, total.transpose(1, 0, 2))


def solution(mesh):
    in_specs = (
        P(("node", "local"), None),
        P(("node", "local"), None),
        P(("node", "local"), None, None),
        P(("node", "local"), None),
    )
    out_specs = (P(("node", "local"), None), P(("node", "local"), None, None))
    return jax.shard_map(body, mesh=mesh, in_specs=in_specs, out_specs=out_specs, check_vma=False)
```

```python
import jax
import jax.numpy as jnp
from jax import lax
from jax.experimental import pallas as pl
from jax.experimental.pallas import tpu as pltpu
from jax.sharding import PartitionSpec as P

AXES = ("node", "local")
X, Y, Z = 0, 1, 2
RING = 4
DEVICES = 128
TILE = 256
BF16 = jnp.bfloat16
F32 = jnp.float32
NT = (((1,), (1,)), ((), ()))
TN = (((0,), (0,)), ((), ()))


def place(device):
    return [device // 64 * 2 + device // 2 % 2, device // 16 % 4, device // 4 % 4, device % 2]


def index(x, y, z, core):
    return (x // 2) * 64 + y * 16 + z * 4 + (x % 2) * 2 + core


def swap(value, axis, wrap):
    pairs = []
    for device in range(DEVICES):
        there = place(device)
        there[axis] = RING - 1 - there[axis] if wrap(there[3]) else there[axis] ^ 1
        pairs.append((device, index(*there)))
    return lax.ppermute(value, AXES, pairs)


def swap_first(value, axis):
    return swap(value, axis, lambda core: core == 1)


def swap_second(value, axis):
    return swap(value, axis, lambda core: core == 0)


def swap_near(value, axis):
    return swap(value, axis, lambda core: False)


def swap_wrap(value, axis):
    return swap(value, axis, lambda core: True)


def swap_corner(value):
    pairs = []
    for device in range(DEVICES):
        there = place(device)
        for axis in (X, Y):
            there[axis] = RING - 1 - there[axis] if there[3] == 1 else there[axis] ^ 1
        pairs.append((device, index(*there)))
    return lax.ppermute(value, AXES, pairs)


def swap_core(value):
    return lax.ppermute(value, AXES, [(d, d ^ 1) for d in range(DEVICES)])


def add(a, b):
    return (a.astype(F32) + b.astype(F32)).astype(BF16)


def join(*blocks):
    return jnp.concatenate(blocks, axis=1)


def gather_block(message):
    return join(message, swap_first(message, Y), swap_first(message, X), swap_corner(message))


def reduce_block(block):
    n = block.shape[1] // 4
    own, along_y, along_x, corner = (block[:, i * n : (i + 1) * n] for i in range(4))
    total = own.astype(F32) + swap_first(along_y, Y).astype(F32)
    return total + swap_first(along_x, X).astype(F32) + swap_corner(corner).astype(F32)


def rows_of(refs, start, stop, cols=slice(None)):
    parts = []
    for ref in refs:
        n = ref.shape[0]
        if start < n and stop > 0:
            parts.append(ref[max(start, 0) : min(stop, n), cols])
        start, stop = start - n, stop - n
    return parts[0] if len(parts) == 1 else jnp.concatenate(parts, axis=0)


def grads_kernel(n, m, parts, *refs):
    xs, cs, refs = refs[:n], refs[n : n + m], refs[n + m :]
    a_ref, hid = refs[-2:]
    ws, befores, gs = refs[:parts], refs[parts : -2 - parts], refs[-2 - parts : -2]
    units, width = ws[0].shape[1:]
    gu = jnp.concatenate([w[m] for w in ws for m in range(2)], axis=0)
    down = jnp.concatenate([w[2] for w in ws], axis=0)
    tokens = hid.shape[1]
    for t in range(tokens // TILE):
        rows = slice(t * TILE, (t + 1) * TILE)
        x = rows_of(xs, t * TILE, (t + 1) * TILE)
        c = rows_of(cs, t * TILE, (t + 1) * TILE)
        z = lax.dot_general(gu, x, NT, preferred_element_type=F32)
        gh = lax.dot_general(down, c, NT, preferred_element_type=F32)
        for p in range(parts):
            gate = z[2 * p * units : (2 * p + 1) * units]
            up = z[(2 * p + 1) * units : (2 * p + 2) * units]
            grad = gh[p * units : (p + 1) * units]
            sg = 1.0 / (1.0 + jnp.exp(-gate))
            silu = gate * sg
            hid[p * units : (p + 1) * units, rows] = (silu * up).astype(BF16)
            slope = sg + silu * (1.0 - sg)
            a_ref[2 * p * units : (2 * p + 1) * units, rows] = (grad * up * slope).astype(BF16)
            a_ref[(2 * p + 1) * units : (2 * p + 2) * units, rows] = (grad * silu).astype(BF16)
    for k in range(width // TILE):
        cols = slice(k * TILE, (k + 1) * TILE)
        x = rows_of(xs, 0, tokens, cols)
        c = rows_of(cs, 0, tokens, cols)
        d_gu = jnp.dot(a_ref[...], x, preferred_element_type=F32)
        d_down = jnp.dot(hid[...], c, preferred_element_type=F32)
        for p, g in enumerate(gs):
            for m in range(3):
                source, row = (d_down, p) if m == 2 else (d_gu, 2 * p + m)
                sums = source[row * units : (row + 1) * units]
                if befores:
                    sums = sums + befores[p][m, :, cols].astype(F32)
                g[m, :, cols] = sums.astype(BF16)


def grads(xs, cs, ws, befores=()):
    units, width = ws[0].shape[1:]
    tokens = sum(x.shape[0] for x in xs)
    vmem = pl.BlockSpec(memory_space=pltpu.VMEM)

    def kernel(*refs):
        grads_kernel(len(xs), len(cs), len(ws), *refs)

    return pl.pallas_call(
        kernel,
        out_shape=[jax.ShapeDtypeStruct(w.shape, BF16) for w in ws]
        + [jax.ShapeDtypeStruct((2 * len(ws) * units, tokens), BF16)],
        in_specs=[vmem] * (len(xs) + len(cs) + len(ws) + len(befores)),
        out_specs=[vmem] * (len(ws) + 1),
        scratch_shapes=[pltpu.VMEM((len(ws) * units, tokens), BF16)],
        compiler_params=pltpu.CompilerParams(vmem_limit_bytes=32 * 1024 * 1024),
        cost_estimate=pl.CostEstimate(
            flops=width if befores else 3 * 10**9, bytes_accessed=width, transcendentals=0
        ),
    )(*xs, *cs, *ws, *befores)


def input_kernel(n, *refs):
    parts, ws = refs[:n], refs[n:-2]
    mine_ref, pair_ref = refs[-2:]
    w_all = jnp.concatenate([w[m] for w in ws for m in range(2)], axis=0)
    group = mine_ref.shape[0]
    for i, ref in enumerate((mine_ref, pair_ref)):
        a = jnp.concatenate([part[:, i * group : (i + 1) * group] for part in parts], axis=0)
        ref[...] = lax.dot_general(a, w_all, TN, preferred_element_type=F32).astype(ref.dtype)


def input_half(parts, ws, group):
    width = ws[0].shape[2]
    vmem = pl.BlockSpec(memory_space=pltpu.VMEM)

    def kernel(*refs):
        input_kernel(len(parts), *refs)

    return pl.pallas_call(
        kernel,
        out_shape=[
            jax.ShapeDtypeStruct((group, width), F32),
            jax.ShapeDtypeStruct((group, width), BF16),
        ],
        in_specs=[vmem] * (len(parts) + len(ws)),
        out_specs=[vmem] * 2,
        compiler_params=pltpu.CompilerParams(vmem_limit_bytes=32 * 1024 * 1024),
        cost_estimate=pl.CostEstimate(
            flops=width, bytes_accessed=width, transcendentals=0
        ),
    )(*parts, *ws)


def body(activations, cotangent, gate_up, down_proj):
    x_z = swap_near(activations, Z)
    message = jnp.concatenate([gate_up.transpose(1, 0, 2), down_proj[None]], axis=0)
    message = lax.optimization_barrier(message)
    block1 = gather_block(swap_wrap(message, Z))
    o0 = gather_block(message)
    block1, c_own = lax.optimization_barrier((block1, cotangent))
    c_z = swap_near(c_own, Z)
    o1, x_z = lax.optimization_barrier((block1, x_z))
    n0, w0 = swap_second(o0, Y), swap_second(o0, X)
    n0, w0 = lax.optimization_barrier((n0, w0))
    n1, w1 = swap_second(o1, X), swap_second(o1, Y)
    n1, w1 = lax.optimization_barrier((n1, w1))
    f0, f1 = swap_second(n0, X), swap_second(n1, Y)
    xs, cs = [activations, swap_core(activations)], [cotangent, swap_core(cotangent)]
    xs_z, cs_z = [x_z, swap_core(x_z)], [c_z, swap_core(c_z)]

    near, far0, far1 = [n1, o1, n0, o0], [f0, w0], [f1, w1]
    *g_near, a_near = grads(xs, cs, near)
    *g_far0, a_far0 = grads(xs, cs, far0)
    f1, a_near, a_far0 = lax.optimization_barrier((f1, a_near, a_far0))
    *g_far1, a_far1 = grads(xs, cs, [f1, w1])
    g_f1, g_w1, a_far1_z = grads(xs_z, cs_z, [f1, w1], g_far1)
    back_f1, back_w1 = swap_second(g_f1, Y), swap_second(g_w1, Y)
    f0, a_far1_z = lax.optimization_barrier((f0, a_far1_z))
    g_f0, g_w0, a_far0_z = grads(xs_z, cs_z, [f0, w0], g_far0)
    back_f0, back_w0 = swap_second(g_f0, X), swap_second(g_w0, X)
    n1, a_far0_z = lax.optimization_barrier((n1, a_far0_z))
    g_n1, g_o1, g_n0, g_o0, a_near_z = grads(xs_z, cs_z, [n1, o1, n0, o0], g_near)

    group = activations.shape[0]
    ws = far1 + far0 + near
    z_part, z_pair = input_half([a_far1_z, a_far0_z, a_near_z], ws, group)
    z_got = swap_core(z_pair)
    mine, pair = input_half([a_far1, a_far0, a_near], ws, group)
    got = swap_core(pair)
    near1 = swap_second(add(g_n1, back_f1), X)
    near0 = swap_second(add(g_n0, back_f0), Y)
    z_part = swap_near((z_part + z_got.astype(F32)).astype(BF16), Z)

    def block_sum(own, back, near):
        return (own.astype(F32) + back.astype(F32) + near.astype(F32)).astype(BF16)

    total1 = reduce_block(block_sum(g_o1, back_w1, near1)).astype(BF16)
    total0 = reduce_block(block_sum(g_o0, back_w0, near0))
    grad_input = (mine + got.astype(F32) + z_part.astype(F32)).astype(BF16)
    total = total0 + swap_wrap(total1, Z).astype(F32)
    return (grad_input, total.transpose(1, 0, 2))


def solution(mesh):
    in_specs = (
        P(("node", "local"), None),
        P(("node", "local"), None),
        P(("node", "local"), None, None),
        P(("node", "local"), None),
    )
    out_specs = (P(("node", "local"), None), P(("node", "local"), None, None))
    return jax.shard_map(body, mesh=mesh, in_specs=in_specs, out_specs=out_specs, check_vma=False)
```

```python
import jax
import jax.numpy as jnp
from jax import lax
from jax.experimental import pallas as pl
from jax.experimental.pallas import tpu as pltpu
from jax.sharding import PartitionSpec as P

AXES = ("node", "local")
X, Y, Z = 0, 1, 2
RING = 4
DEVICES = 128
TILE = 256
BF16 = jnp.bfloat16
F32 = jnp.float32
NT = (((1,), (1,)), ((), ()))
TN = (((0,), (0,)), ((), ()))


def place(device):
    return [device // 64 * 2 + device // 2 % 2, device // 16 % 4, device // 4 % 4, device % 2]


def index(x, y, z, core):
    return (x // 2) * 64 + y * 16 + z * 4 + (x % 2) * 2 + core


def swap(value, axis, wrap):
    pairs = []
    for device in range(DEVICES):
        there = place(device)
        there[axis] = RING - 1 - there[axis] if wrap(there[3]) else there[axis] ^ 1
        pairs.append((device, index(*there)))
    return lax.ppermute(value, AXES, pairs)


def swap_first(value, axis):
    return swap(value, axis, lambda core: core == 1)


def swap_second(value, axis):
    return swap(value, axis, lambda core: core == 0)


def swap_near(value, axis):
    return swap(value, axis, lambda core: False)


def swap_wrap(value, axis):
    return swap(value, axis, lambda core: True)


def swap_corner(value):
    pairs = []
    for device in range(DEVICES):
        there = place(device)
        for axis in (X, Y):
            there[axis] = RING - 1 - there[axis] if there[3] == 1 else there[axis] ^ 1
        pairs.append((device, index(*there)))
    return lax.ppermute(value, AXES, pairs)


def swap_core(value):
    return lax.ppermute(value, AXES, [(d, d ^ 1) for d in range(DEVICES)])


def add(a, b):
    return (a.astype(F32) + b.astype(F32)).astype(BF16)


def join(*blocks):
    return jnp.concatenate(blocks, axis=1)


def gather_block(message):
    return join(message, swap_first(message, Y), swap_first(message, X), swap_corner(message))


def reduce_block(block):
    n = block.shape[1] // 4
    own, along_y, along_x, corner = (block[:, i * n : (i + 1) * n] for i in range(4))
    total = own.astype(F32) + swap_first(along_y, Y).astype(F32)
    return total + swap_first(along_x, X).astype(F32) + swap_corner(corner).astype(F32)


def rows_of(refs, start, stop, cols=slice(None)):
    parts = []
    for ref in refs:
        n = ref.shape[0]
        if start < n and stop > 0:
            parts.append(ref[max(start, 0) : min(stop, n), cols])
        start, stop = start - n, stop - n
    return parts[0] if len(parts) == 1 else jnp.concatenate(parts, axis=0)


def grads_kernel(n, m, parts, joined, *refs):
    xs, cs, refs = refs[:n], refs[n : n + m], refs[n + m :]
    a_ref, hid = refs[-2:]
    outs = parts // joined
    ws, befores, gs = refs[:parts], refs[parts : -2 - outs], refs[-2 - outs : -2]
    units, width = ws[0].shape[1:]
    gu = jnp.concatenate([w[m] for w in ws for m in range(2)], axis=0)
    down = jnp.concatenate([w[2] for w in ws], axis=0)
    tokens = hid.shape[1]
    for t in range(tokens // TILE):
        rows = slice(t * TILE, (t + 1) * TILE)
        x = rows_of(xs, t * TILE, (t + 1) * TILE)
        c = rows_of(cs, t * TILE, (t + 1) * TILE)
        z = lax.dot_general(gu, x, NT, preferred_element_type=F32)
        gh = lax.dot_general(down, c, NT, preferred_element_type=F32)
        for p in range(parts):
            gate = z[2 * p * units : (2 * p + 1) * units]
            up = z[(2 * p + 1) * units : (2 * p + 2) * units]
            grad = gh[p * units : (p + 1) * units]
            sg = 1.0 / (1.0 + jnp.exp(-gate))
            silu = gate * sg
            hid[p * units : (p + 1) * units, rows] = (silu * up).astype(BF16)
            slope = sg + silu * (1.0 - sg)
            a_ref[2 * p * units : (2 * p + 1) * units, rows] = (grad * up * slope).astype(BF16)
            a_ref[(2 * p + 1) * units : (2 * p + 2) * units, rows] = (grad * silu).astype(BF16)
    for k in range(width // TILE):
        cols = slice(k * TILE, (k + 1) * TILE)
        x = rows_of(xs, 0, tokens, cols)
        c = rows_of(cs, 0, tokens, cols)
        d_gu = jnp.dot(a_ref[...], x, preferred_element_type=F32)
        d_down = jnp.dot(hid[...], c, preferred_element_type=F32)
        for p in range(parts):
            g, before = gs[p // joined], befores[p // joined] if befores else None
            to = slice(p % joined * units, (p % joined + 1) * units)
            for m in range(3):
                source, row = (d_down, p) if m == 2 else (d_gu, 2 * p + m)
                sums = source[row * units : (row + 1) * units]
                if before is not None:
                    sums = sums + before[m, to, cols].astype(F32)
                g[m, to, cols] = sums.astype(BF16)


def grads(xs, cs, ws, befores=(), joined=1, weight=0):
    units, width = ws[0].shape[1:]
    tokens = sum(x.shape[0] for x in xs)
    vmem = pl.BlockSpec(memory_space=pltpu.VMEM)

    def kernel(*refs):
        grads_kernel(len(xs), len(cs), len(ws), joined, *refs)

    return pl.pallas_call(
        kernel,
        out_shape=[jax.ShapeDtypeStruct((3, joined * units, width), BF16)] * (len(ws) // joined)
        + [jax.ShapeDtypeStruct((2 * len(ws) * units, tokens), BF16)],
        in_specs=[vmem] * (len(xs) + len(cs) + len(ws) + len(befores)),
        out_specs=[vmem] * (len(ws) // joined + 1),
        scratch_shapes=[pltpu.VMEM((len(ws) * units, tokens), BF16)],
        compiler_params=pltpu.CompilerParams(vmem_limit_bytes=32 * 1024 * 1024),
        cost_estimate=pl.CostEstimate(
            flops=width + weight * 10**9, bytes_accessed=width, transcendentals=0
        ),
    )(*xs, *cs, *ws, *befores)


def input_kernel(n, *refs):
    parts, ws = refs[:n], refs[n:-4]
    outs = refs[-4:]
    w_all = jnp.concatenate([w[m] for w in ws for m in range(2)], axis=0)
    group = outs[0].shape[0]
    k = len(parts) // 2
    for i in range(4):
        half = parts[i // 2 * k : (i // 2 + 1) * k]
        a = jnp.concatenate([part[:, i % 2 * group : (i % 2 + 1) * group] for part in half], axis=0)
        total = lax.dot_general(a, w_all, TN, preferred_element_type=F32)
        outs[i][...] = total.astype(outs[i].dtype)


def input_parts(parts, ws):
    width = ws[0].shape[2]
    group = parts[0].shape[1] // 2
    vmem = pl.BlockSpec(memory_space=pltpu.VMEM)

    def kernel(*refs):
        input_kernel(len(parts), *refs)

    return pl.pallas_call(
        kernel,
        out_shape=[
            jax.ShapeDtypeStruct((group, width), kind) for kind in (F32, BF16, F32, BF16)
        ],
        in_specs=[vmem] * (len(parts) + len(ws)),
        out_specs=[vmem] * 4,
        compiler_params=pltpu.CompilerParams(vmem_limit_bytes=32 * 1024 * 1024),
        cost_estimate=pl.CostEstimate(
            flops=width, bytes_accessed=width, transcendentals=0
        ),
    )(*parts, *ws)


def body(activations, cotangent, gate_up, down_proj):
    x_z = swap_near(activations, Z)
    message = jnp.concatenate([gate_up.transpose(1, 0, 2), down_proj[None]], axis=0)
    message = lax.optimization_barrier(message)
    other = swap_wrap(message, Z)
    block1 = gather_block(other)
    o0, _ = lax.optimization_barrier((gather_block(message), other))
    block1, c_own = lax.optimization_barrier((block1, cotangent))
    c_z = swap_near(c_own, Z)
    o1, x_z = lax.optimization_barrier((block1, x_z))
    n0, w0 = swap_second(o0, Y), swap_second(o0, X)
    n1 = swap_second(o1, X)
    w1 = swap_second(o1, Y)
    f0, f1 = swap_second(n0, X), swap_second(n1, Y)
    xs, cs = [activations, swap_core(activations)], [cotangent, swap_core(cotangent)]

    near = [n1, o1, n0, o0]
    *g_near, a_near = grads(xs, cs, near, weight=3)
    x_z, c_z, a_near = lax.optimization_barrier((x_z, c_z, a_near))
    xs_z, cs_z = [x_z, swap_core(x_z)], [c_z, swap_core(c_z)]
    f0, w1 = lax.optimization_barrier((f0, w1))
    g_r0, a_r0 = grads(xs, cs, [w0, f0], joined=2, weight=0)
    f1, a_r0 = lax.optimization_barrier((f1, a_r0))
    g_r1, a_r1 = grads(xs, cs, [w1, f1], joined=2, weight=3)

    g_r1, a_r1_z = grads(xs_z, cs_z, [w1, f1], [g_r1], joined=2)
    back1 = swap_second(g_r1, Y)
    f0, a_r1_z = lax.optimization_barrier((f0, a_r1_z))
    g_r0, a_r0_z = grads(xs_z, cs_z, [w0, f0], [g_r0], joined=2)
    back0 = swap_second(g_r0, X)
    n1, a_r0_z = lax.optimization_barrier((n1, a_r0_z))
    g_n1, g_o1, g_n0, g_o0, a_near_z = grads(xs_z, cs_z, [n1, o1, n0, o0], g_near)
    parts = [a_r1, a_r0, a_near, a_r1_z, a_r0_z, a_near_z]
    own, pair, z_part, z_pair = input_parts(parts, [w1, f1, w0, f0] + near)
    z_got, got = swap_core(z_pair), swap_core(pair)

    n = g_n1.shape[1]
    near1 = swap_second(add(g_n1, back1[:, n:]), X)
    back0, back1 = lax.optimization_barrier((back0, back1))
    near0 = swap_second(add(g_n0, back0[:, n:]), Y)
    back0, z_part = lax.optimization_barrier((back0, z_part))
    mine = own + got.astype(F32)
    z_part = swap_near((z_part + z_got.astype(F32)).astype(BF16), Z)

    def block_sum(own, back, near):
        return (own.astype(F32) + back.astype(F32) + near.astype(F32)).astype(BF16)

    total1 = reduce_block(block_sum(g_o1, back1[:, :n], near1)).astype(BF16)
    total0 = reduce_block(block_sum(g_o0, back0[:, :n], near0))
    grad_input = (mine + z_part.astype(F32)).astype(BF16)
    total = total0 + swap_wrap(total1, Z).astype(F32)
    return (grad_input, total.transpose(1, 0, 2))


def solution(mesh):
    in_specs = (
        P(("node", "local"), None),
        P(("node", "local"), None),
        P(("node", "local"), None, None),
        P(("node", "local"), None),
    )
    out_specs = (P(("node", "local"), None), P(("node", "local"), None, None))
    return jax.shard_map(body, mesh=mesh, in_specs=in_specs, out_specs=out_specs, check_vma=False)
```

```python
import jax
import jax.numpy as jnp
from jax import lax
from jax.experimental import pallas as pl
from jax.experimental.pallas import tpu as pltpu
from jax.sharding import PartitionSpec as P

AXES = ("node", "local")
X, Y, Z = 0, 1, 2
RING = 4
DEVICES = 128
TILE = 256
BF16 = jnp.bfloat16
F32 = jnp.float32
NT = (((1,), (1,)), ((), ()))
TN = (((0,), (0,)), ((), ()))


def place(device):
    return [device // 64 * 2 + device // 2 % 2, device // 16 % 4, device // 4 % 4, device % 2]


def index(x, y, z, core):
    return (x // 2) * 64 + y * 16 + z * 4 + (x % 2) * 2 + core


def swap(value, axis, wrap):
    pairs = []
    for device in range(DEVICES):
        there = place(device)
        there[axis] = RING - 1 - there[axis] if wrap(there[3]) else there[axis] ^ 1
        pairs.append((device, index(*there)))
    return lax.ppermute(value, AXES, pairs)


def swap_first(value, axis):
    return swap(value, axis, lambda core: core == 1)


def swap_second(value, axis):
    return swap(value, axis, lambda core: core == 0)


def swap_near(value, axis):
    return swap(value, axis, lambda core: False)


def swap_wrap(value, axis):
    return swap(value, axis, lambda core: True)


def blocks_of_four():
    groups = {}
    for device in range(DEVICES):
        x, y, z, core = place(device)
        key = z, core, (x + core) % RING // 2, (y + core) % RING // 2
        groups.setdefault(key, []).append(device)
    return list(groups.values())


def trade(pieces):
    return lax.all_to_all(pieces, AXES, 0, 0, axis_index_groups=blocks_of_four(), tiled=True)


def swap_core(value):
    return lax.ppermute(value, AXES, [(d, d ^ 1) for d in range(DEVICES)])


def add(a, b):
    return (a.astype(F32) + b.astype(F32)).astype(BF16)


def join(*blocks):
    return jnp.concatenate(blocks, axis=1)


def gather_block(message):
    got = trade(jnp.broadcast_to(message[None], (4,) + message.shape))
    return got.transpose(1, 0, 2, 3).reshape(message.shape[0], -1, message.shape[2])


def reduce_block(block):
    mats, rows, width = block.shape
    pieces = block.reshape(mats, 4, rows // 4, width).transpose(1, 0, 2, 3)
    return jnp.sum(trade(pieces).astype(F32), axis=0)


def halve(both, axis):
    n = both.shape[1] // 2
    return add(both[:, :n], swap_second(both[:, n:], axis))


def rows_of(refs, start, stop, cols=slice(None)):
    parts = []
    for ref in refs:
        n = ref.shape[0]
        if start < n and stop > 0:
            parts.append(ref[max(start, 0) : min(stop, n), cols])
        start, stop = start - n, stop - n
    return parts[0] if len(parts) == 1 else jnp.concatenate(parts, axis=0)


def grads_kernel(n, *refs):
    xs, cs, refs = refs[:n], refs[n : 2 * n], refs[2 * n :]
    a_ref, hid = refs[-2:]
    parts = len(refs) // 2 - 1
    ws, gs = refs[:parts], refs[parts:-2]
    units, width = ws[0].shape[1:]
    gu = jnp.concatenate([w[m] for w in ws for m in range(2)], axis=0)
    down = jnp.concatenate([w[2] for w in ws], axis=0)
    tokens = hid.shape[1]
    for t in range(tokens // TILE):
        rows = slice(t * TILE, (t + 1) * TILE)
        x = rows_of(xs, t * TILE, (t + 1) * TILE)
        c = rows_of(cs, t * TILE, (t + 1) * TILE)
        z = lax.dot_general(gu, x, NT, preferred_element_type=F32)
        gh = lax.dot_general(down, c, NT, preferred_element_type=F32)
        for p in range(parts):
            gate = z[2 * p * units : (2 * p + 1) * units]
            up = z[(2 * p + 1) * units : (2 * p + 2) * units]
            grad = gh[p * units : (p + 1) * units]
            sg = 1.0 / (1.0 + jnp.exp(-gate))
            silu = gate * sg
            hid[p * units : (p + 1) * units, rows] = (silu * up).astype(BF16)
            slope = sg + silu * (1.0 - sg)
            a_ref[2 * p * units : (2 * p + 1) * units, rows] = (grad * up * slope).astype(BF16)
            a_ref[(2 * p + 1) * units : (2 * p + 2) * units, rows] = (grad * silu).astype(BF16)
    for k in range(width // TILE):
        cols = slice(k * TILE, (k + 1) * TILE)
        x = rows_of(xs, 0, tokens, cols)
        c = rows_of(cs, 0, tokens, cols)
        d_gu = jnp.dot(a_ref[...], x, preferred_element_type=F32).astype(BF16)
        d_down = jnp.dot(hid[...], c, preferred_element_type=F32).astype(BF16)
        for p, g in enumerate(gs):
            for m in range(2):
                g[m, :, cols] = d_gu[(2 * p + m) * units : (2 * p + m + 1) * units]
            g[2, :, cols] = d_down[p * units : (p + 1) * units]


def grads(xs, cs, ws):
    units, width = ws[0].shape[1:]
    tokens = sum(x.shape[0] for x in xs)
    vmem = pl.BlockSpec(memory_space=pltpu.VMEM)

    def kernel(*refs):
        grads_kernel(len(xs), *refs)

    return pl.pallas_call(
        kernel,
        out_shape=[jax.ShapeDtypeStruct(w.shape, BF16) for w in ws]
        + [jax.ShapeDtypeStruct((2 * len(ws) * units, tokens), BF16)],
        in_specs=[vmem] * (2 * len(xs) + len(ws)),
        out_specs=[vmem] * (len(ws) + 1),
        scratch_shapes=[pltpu.VMEM((len(ws) * units, tokens), BF16)],
        compiler_params=pltpu.CompilerParams(vmem_limit_bytes=32 * 1024 * 1024),
        cost_estimate=pl.CostEstimate(
            flops=width, bytes_accessed=width, transcendentals=0
        ),
    )(*xs, *cs, *ws)


def input_kernel(n, *refs):
    parts, ws = refs[:n], refs[n:-3]
    own_ref, z_ref, pair_ref = refs[-3:]
    w_all = jnp.concatenate([w[m] for w in ws for m in range(2)], axis=0)
    group = own_ref.shape[0]
    for i in range(4):
        cols = slice(i * group, (i + 1) * group)
        a = jnp.concatenate([part[:, cols] for part in parts], axis=0)
        total = lax.dot_general(a, w_all, TN, preferred_element_type=F32)
        if i == 0:
            own_ref[...] = total
        elif i == 2:
            z_ref[...] = total
        else:
            pair_ref[i // 2] = total.astype(BF16)


def input_parts(parts, ws):
    units, width = ws[0].shape[1:]
    group = parts[0].shape[1] // 4
    vmem = pl.BlockSpec(memory_space=pltpu.VMEM)

    def kernel(*refs):
        input_kernel(len(parts), *refs)

    return pl.pallas_call(
        kernel,
        out_shape=[
            jax.ShapeDtypeStruct((group, width), F32),
            jax.ShapeDtypeStruct((group, width), F32),
            jax.ShapeDtypeStruct((2, group, width), BF16),
        ],
        in_specs=[vmem] * (len(parts) + len(ws)),
        out_specs=[vmem] * 3,
        compiler_params=pltpu.CompilerParams(vmem_limit_bytes=32 * 1024 * 1024),
        cost_estimate=pl.CostEstimate(
            flops=width, bytes_accessed=width, transcendentals=0
        ),
    )(*parts, *ws)


def body(activations, cotangent, gate_up, down_proj):
    x_z = swap_near(activations, Z)
    message = jnp.concatenate([gate_up.transpose(1, 0, 2), down_proj[None]], axis=0)
    other = swap_wrap(message, Z)
    block0 = gather_block(message)
    block1 = gather_block(other)
    block1, x_z, c_own = lax.optimization_barrier((block1, x_z, cotangent))
    c_z = swap_near(c_own, Z)
    j0 = join(block0, swap_second(block0, Y))
    j1 = join(block1, swap_second(block1, X))
    r0, r1 = swap_second(j0, X), swap_second(j1, Y)
    xs = [activations, swap_core(activations), x_z, swap_core(x_z)]
    cs = [cotangent, swap_core(cotangent), c_z, swap_core(c_z)]

    g_r0, a_r0 = grads(xs, cs, [r0])
    back0 = swap_second(g_r0, X)
    g_r1, a_r1 = grads(xs, cs, [r1])
    back1 = swap_second(g_r1, Y)
    j0, j1, a_r1 = lax.optimization_barrier((j0, j1, a_r1))
    g_j0, g_j1, a_j = grads(xs, cs, [j0, j1])

    own, z_part, pair = input_parts([a_r0, a_r1, a_j], [r0, r1, j0, j1])
    got = swap_core(pair)
    near0, near1 = add(g_j0, back0), add(g_j1, back1)
    near0, near1, z_part = lax.optimization_barrier((near0, near1, z_part))
    mine = own + got[0].astype(F32)
    z_part = swap_near((z_part + got[1].astype(F32)).astype(BF16), Z)

    total1 = reduce_block(halve(near1, X)).astype(BF16)
    total1, z_part = lax.optimization_barrier((total1, z_part))
    grad_input = (mine + z_part.astype(F32)).astype(BF16)
    total0 = reduce_block(halve(near0, Y))
    total = total0 + swap_wrap(total1, Z).astype(F32)
    return (grad_input, total.transpose(1, 0, 2))


def solution(mesh):
    in_specs = (
        P(("node", "local"), None),
        P(("node", "local"), None),
        P(("node", "local"), None, None),
        P(("node", "local"), None),
    )
    out_specs = (P(("node", "local"), None), P(("node", "local"), None, None))
    return jax.shard_map(body, mesh=mesh, in_specs=in_specs, out_specs=out_specs, check_vma=False)
```

```python
import jax
import jax.numpy as jnp
from jax import lax
from jax.experimental import pallas as pl
from jax.experimental.pallas import tpu as pltpu
from jax.sharding import PartitionSpec as P

AXES = ("node", "local")
X, Y, Z = 0, 1, 2
RING = 4
DEVICES = 128
TILE = 256
BF16 = jnp.bfloat16
F32 = jnp.float32
NT = (((1,), (1,)), ((), ()))
TN = (((0,), (0,)), ((), ()))


def place(device):
    return [device // 64 * 2 + device // 2 % 2, device // 16 % 4, device // 4 % 4, device % 2]


def index(x, y, z, core):
    return (x // 2) * 64 + y * 16 + z * 4 + (x % 2) * 2 + core


def swap(value, axis, wrap):
    pairs = []
    for device in range(DEVICES):
        there = place(device)
        there[axis] = RING - 1 - there[axis] if wrap(there[3]) else there[axis] ^ 1
        pairs.append((device, index(*there)))
    return lax.ppermute(value, AXES, pairs)


def swap_first(value, axis):
    return swap(value, axis, lambda core: core == 1)


def swap_second(value, axis):
    return swap(value, axis, lambda core: core == 0)


def swap_near(value, axis):
    return swap(value, axis, lambda core: False)


def swap_wrap(value, axis):
    return swap(value, axis, lambda core: True)


def swap_corner(value):
    pairs = []
    for device in range(DEVICES):
        there = place(device)
        for axis in (X, Y):
            there[axis] = RING - 1 - there[axis] if there[3] == 1 else there[axis] ^ 1
        pairs.append((device, index(*there)))
    return lax.ppermute(value, AXES, pairs)


def swap_core(value):
    return lax.ppermute(value, AXES, [(d, d ^ 1) for d in range(DEVICES)])


def add(a, b):
    return (a.astype(F32) + b.astype(F32)).astype(BF16)


def join(*blocks):
    return jnp.concatenate(blocks, axis=1)


def gather_block(message):
    return join(message, swap_first(message, Y), swap_first(message, X), swap_corner(message))


def reduce_block(block):
    n = block.shape[1] // 4
    own, along_y, along_x, corner = (block[:, i * n : (i + 1) * n] for i in range(4))
    return own, swap_first(along_y, Y), swap_first(along_x, X), swap_corner(corner)


def added(terms):
    return sum(term.astype(F32) for term in terms)


def rows_of(refs, start, stop, cols=slice(None)):
    parts = []
    for ref in refs:
        n = ref.shape[0]
        if start < n and stop > 0:
            parts.append(ref[max(start, 0) : min(stop, n), cols])
        start, stop = start - n, stop - n
    return parts[0] if len(parts) == 1 else jnp.concatenate(parts, axis=0)


def grads_kernel(n, m, parts, joined, *refs):
    xs, cs, refs = refs[:n], refs[n : n + m], refs[n + m :]
    a_ref, hid = refs[-2:]
    outs = parts // joined
    ws, befores, gs = refs[:parts], refs[parts : -2 - outs], refs[-2 - outs : -2]
    units, width = ws[0].shape[1:]
    gu = jnp.concatenate([w[m] for w in ws for m in range(2)], axis=0)
    down = jnp.concatenate([w[2] for w in ws], axis=0)
    tokens = hid.shape[1]
    for t in range(tokens // TILE):
        rows = slice(t * TILE, (t + 1) * TILE)
        x = rows_of(xs, t * TILE, (t + 1) * TILE)
        c = rows_of(cs, t * TILE, (t + 1) * TILE)
        z = lax.dot_general(gu, x, NT, preferred_element_type=F32)
        gh = lax.dot_general(down, c, NT, preferred_element_type=F32)
        for p in range(parts):
            gate = z[2 * p * units : (2 * p + 1) * units]
            up = z[(2 * p + 1) * units : (2 * p + 2) * units]
            grad = gh[p * units : (p + 1) * units]
            sg = 1.0 / (1.0 + jnp.exp(-gate))
            silu = gate * sg
            hid[p * units : (p + 1) * units, rows] = (silu * up).astype(BF16)
            slope = sg + silu * (1.0 - sg)
            a_ref[2 * p * units : (2 * p + 1) * units, rows] = (grad * up * slope).astype(BF16)
            a_ref[(2 * p + 1) * units : (2 * p + 2) * units, rows] = (grad * silu).astype(BF16)
    for k in range(width // TILE):
        cols = slice(k * TILE, (k + 1) * TILE)
        x = rows_of(xs, 0, tokens, cols)
        c = rows_of(cs, 0, tokens, cols)
        d_gu = jnp.dot(a_ref[...], x, preferred_element_type=F32)
        d_down = jnp.dot(hid[...], c, preferred_element_type=F32)
        for p in range(parts):
            g, before = gs[p // joined], befores[p // joined] if befores else None
            to = slice(p % joined * units, (p % joined + 1) * units)
            for m in range(3):
                source, row = (d_down, p) if m == 2 else (d_gu, 2 * p + m)
                sums = source[row * units : (row + 1) * units]
                if before is not None:
                    sums = sums + before[m, to, cols].astype(F32)
                g[m, to, cols] = sums.astype(BF16)


def grads(xs, cs, ws, befores=(), joined=1, weight=0):
    units, width = ws[0].shape[1:]
    tokens = sum(x.shape[0] for x in xs)
    vmem = pl.BlockSpec(memory_space=pltpu.VMEM)

    def kernel(*refs):
        grads_kernel(len(xs), len(cs), len(ws), joined, *refs)

    return pl.pallas_call(
        kernel,
        out_shape=[jax.ShapeDtypeStruct((3, joined * units, width), BF16)] * (len(ws) // joined)
        + [jax.ShapeDtypeStruct((2 * len(ws) * units, tokens), BF16)],
        in_specs=[vmem] * (len(xs) + len(cs) + len(ws) + len(befores)),
        out_specs=[vmem] * (len(ws) // joined + 1),
        scratch_shapes=[pltpu.VMEM((len(ws) * units, tokens), BF16)],
        compiler_params=pltpu.CompilerParams(vmem_limit_bytes=32 * 1024 * 1024),
        cost_estimate=pl.CostEstimate(
            flops=width + weight * 10**9, bytes_accessed=width, transcendentals=0
        ),
    )(*xs, *cs, *ws, *befores)


def input_kernel(n, *refs):
    parts, ws = refs[:n], refs[n:-4]
    outs = refs[-4:]
    w_all = jnp.concatenate([w[m] for w in ws for m in range(2)], axis=0)
    group = outs[0].shape[0]
    k = len(parts) // 2
    for i in range(4):
        half = parts[i // 2 * k : (i // 2 + 1) * k]
        a = jnp.concatenate([part[:, i % 2 * group : (i % 2 + 1) * group] for part in half], axis=0)
        total = lax.dot_general(a, w_all, TN, preferred_element_type=F32)
        outs[i][...] = total.astype(outs[i].dtype)


def input_parts(parts, ws):
    width = ws[0].shape[2]
    group = parts[0].shape[1] // 2
    vmem = pl.BlockSpec(memory_space=pltpu.VMEM)

    def kernel(*refs):
        input_kernel(len(parts), *refs)

    return pl.pallas_call(
        kernel,
        out_shape=[
            jax.ShapeDtypeStruct((group, width), kind) for kind in (F32, BF16, F32, BF16)
        ],
        in_specs=[vmem] * (len(parts) + len(ws)),
        out_specs=[vmem] * 4,
        compiler_params=pltpu.CompilerParams(vmem_limit_bytes=32 * 1024 * 1024),
        cost_estimate=pl.CostEstimate(
            flops=width, bytes_accessed=width, transcendentals=0
        ),
    )(*parts, *ws)


def body(activations, cotangent, gate_up, down_proj):
    x_z = swap_near(activations, Z)
    message = jnp.concatenate([gate_up.transpose(1, 0, 2), down_proj[None]], axis=0)
    message = lax.optimization_barrier(message)
    block1 = gather_block(swap_wrap(message, Z))
    o0 = gather_block(message)
    block1, c_own = lax.optimization_barrier((block1, cotangent))
    c_z = swap_near(c_own, Z)
    o1, x_z = lax.optimization_barrier((block1, x_z))
    n0 = swap_second(o0, Y)
    r0 = swap_second(join(o0, n0), X)
    n1 = swap_second(o1, X)
    w1 = swap_second(o1, Y)
    f1 = swap_second(n1, Y)
    xs, cs = [activations, swap_core(activations)], [cotangent, swap_core(cotangent)]

    near = [n1, o1, n0, o0]
    *g_near, a_near = grads(xs, cs, near, weight=3)
    x_z, c_z, a_near, w1 = lax.optimization_barrier((x_z, c_z, a_near, w1))
    xs_z, cs_z = [x_z, swap_core(x_z)], [c_z, swap_core(c_z)]
    f1, a_near = lax.optimization_barrier((f1, a_near))
    g_r1, a_r1 = grads(xs, cs, [w1, f1], joined=2, weight=6)

    g_r1, a_r1_z = grads(xs_z, cs_z, [w1, f1], [g_r1], joined=2)
    back1 = swap_second(g_r1, Y)
    r0, a_r1_z = lax.optimization_barrier((r0, a_r1_z))
    g_r0, a_r0 = grads(xs + xs_z, cs + cs_z, [r0])
    back0 = swap_second(g_r0, X)
    n1, a_r0 = lax.optimization_barrier((n1, a_r0))
    g_n1, g_o1, g_n0, g_o0, a_near_z = grads(xs_z, cs_z, [n1, o1, n0, o0], g_near)
    n = a_r0.shape[1] // 2
    parts = [a_r1, a_r0[:, :n], a_near, a_r1_z, a_r0[:, n:], a_near_z]
    own, pair, z_part, z_pair = input_parts(parts, [w1, f1, r0] + near)
    z_got, got = swap_core(z_pair), swap_core(pair)

    n = g_n1.shape[1]
    near1 = swap_second(add(g_n1, back1[:, n:]), X)
    back0, back1 = lax.optimization_barrier((back0, back1))
    near0 = swap_second(add(g_n0, back0[:, n:]), Y)
    back0, z_part = lax.optimization_barrier((back0, z_part))
    mine = own + got.astype(F32)
    z_part = swap_near((z_part + z_got.astype(F32)).astype(BF16), Z)

    def block_sum(own, back, near):
        return (own.astype(F32) + back.astype(F32) + near.astype(F32)).astype(BF16)

    terms1 = reduce_block(block_sum(g_o1, back1[:, :n], near1))
    total1 = added(terms1).astype(BF16)
    total0 = added(reduce_block(block_sum(g_o0, back0[:, :n], near0)))
    grad_input = (mine + z_part.astype(F32)).astype(BF16)
    total = total0 + swap_wrap(total1, Z).astype(F32)
    return (grad_input, total.transpose(1, 0, 2))


def solution(mesh):
    in_specs = (
        P(("node", "local"), None),
        P(("node", "local"), None),
        P(("node", "local"), None, None),
        P(("node", "local"), None),
    )
    out_specs = (P(("node", "local"), None), P(("node", "local"), None, None))
    return jax.shard_map(body, mesh=mesh, in_specs=in_specs, out_specs=out_specs, check_vma=False)
```

```python
import jax
import jax.numpy as jnp
from jax import lax
from jax.experimental import pallas as pl
from jax.experimental.pallas import tpu as pltpu
from jax.sharding import PartitionSpec as P

AXES = ("node", "local")
X, Y, Z = 0, 1, 2
RING = 4
DEVICES = 128
TILE = 256
BF16 = jnp.bfloat16
F32 = jnp.float32
NT = (((1,), (1,)), ((), ()))
TN = (((0,), (0,)), ((), ()))


def place(device):
    return [device // 64 * 2 + device // 2 % 2, device // 16 % 4, device // 4 % 4, device % 2]


def index(x, y, z, core):
    return (x // 2) * 64 + y * 16 + z * 4 + (x % 2) * 2 + core


def swap(value, axis, wrap):
    pairs = []
    for device in range(DEVICES):
        there = place(device)
        there[axis] = RING - 1 - there[axis] if wrap(there[3]) else there[axis] ^ 1
        pairs.append((device, index(*there)))
    return lax.ppermute(value, AXES, pairs)


def swap_first(value, axis):
    return swap(value, axis, lambda core: core == 1)


def swap_second(value, axis):
    return swap(value, axis, lambda core: core == 0)


def swap_near(value, axis):
    return swap(value, axis, lambda core: False)


def swap_wrap(value, axis):
    return swap(value, axis, lambda core: True)


def swap_corner(value):
    pairs = []
    for device in range(DEVICES):
        there = place(device)
        for axis in (X, Y):
            there[axis] = RING - 1 - there[axis] if there[3] == 1 else there[axis] ^ 1
        pairs.append((device, index(*there)))
    return lax.ppermute(value, AXES, pairs)


def swap_core(value):
    return lax.ppermute(value, AXES, [(d, d ^ 1) for d in range(DEVICES)])


def add(a, b):
    return (a.astype(F32) + b.astype(F32)).astype(BF16)


def join(*blocks):
    return jnp.concatenate(blocks, axis=1)


def gather_block(message):
    return join(message, swap_first(message, Y), swap_first(message, X), swap_corner(message))


def reduce_block(block):
    n = block.shape[1] // 4
    own, along_y, along_x, corner = (block[:, i * n : (i + 1) * n] for i in range(4))
    return own, swap_first(along_y, Y), swap_first(along_x, X), swap_corner(corner)


def added(terms):
    return sum(term.astype(F32) for term in terms)


def rows_of(refs, start, stop, cols=slice(None)):
    parts = []
    for ref in refs:
        n = ref.shape[0]
        if start < n and stop > 0:
            parts.append(ref[max(start, 0) : min(stop, n), cols])
        start, stop = start - n, stop - n
    return parts[0] if len(parts) == 1 else jnp.concatenate(parts, axis=0)


def grads_kernel(n, m, parts, joined, *refs):
    xs, cs, refs = refs[:n], refs[n : n + m], refs[n + m :]
    a_ref, hid = refs[-2:]
    outs = parts // joined
    ws, befores, gs = refs[:parts], refs[parts : -2 - outs], refs[-2 - outs : -2]
    units, width = ws[0].shape[1:]
    gu = jnp.concatenate([w[m] for w in ws for m in range(2)], axis=0)
    down = jnp.concatenate([w[2] for w in ws], axis=0)
    tokens = hid.shape[1]
    for t in range(tokens // TILE):
        rows = slice(t * TILE, (t + 1) * TILE)
        x = rows_of(xs, t * TILE, (t + 1) * TILE)
        c = rows_of(cs, t * TILE, (t + 1) * TILE)
        z = lax.dot_general(gu, x, NT, preferred_element_type=F32)
        gh = lax.dot_general(down, c, NT, preferred_element_type=F32)
        for p in range(parts):
            gate = z[2 * p * units : (2 * p + 1) * units]
            up = z[(2 * p + 1) * units : (2 * p + 2) * units]
            grad = gh[p * units : (p + 1) * units]
            sg = 1.0 / (1.0 + jnp.exp(-gate))
            silu = gate * sg
            hid[p * units : (p + 1) * units, rows] = (silu * up).astype(BF16)
            slope = sg + silu * (1.0 - sg)
            a_ref[2 * p * units : (2 * p + 1) * units, rows] = (grad * up * slope).astype(BF16)
            a_ref[(2 * p + 1) * units : (2 * p + 2) * units, rows] = (grad * silu).astype(BF16)
    for k in range(width // TILE):
        cols = slice(k * TILE, (k + 1) * TILE)
        x = rows_of(xs, 0, tokens, cols)
        c = rows_of(cs, 0, tokens, cols)
        d_gu = jnp.dot(a_ref[...], x, preferred_element_type=F32)
        d_down = jnp.dot(hid[...], c, preferred_element_type=F32)
        for p in range(parts):
            g, before = gs[p // joined], befores[p // joined] if befores else None
            to = slice(p % joined * units, (p % joined + 1) * units)
            for m in range(3):
                source, row = (d_down, p) if m == 2 else (d_gu, 2 * p + m)
                sums = source[row * units : (row + 1) * units]
                if before is not None:
                    sums = sums + before[m, to, cols].astype(F32)
                g[m, to, cols] = sums.astype(BF16)


def grads(xs, cs, ws, befores=(), joined=1, weight=0):
    units, width = ws[0].shape[1:]
    tokens = sum(x.shape[0] for x in xs)
    vmem = pl.BlockSpec(memory_space=pltpu.VMEM)

    def kernel(*refs):
        grads_kernel(len(xs), len(cs), len(ws), joined, *refs)

    return pl.pallas_call(
        kernel,
        out_shape=[jax.ShapeDtypeStruct((3, joined * units, width), BF16)] * (len(ws) // joined)
        + [jax.ShapeDtypeStruct((2 * len(ws) * units, tokens), BF16)],
        in_specs=[vmem] * (len(xs) + len(cs) + len(ws) + len(befores)),
        out_specs=[vmem] * (len(ws) // joined + 1),
        scratch_shapes=[pltpu.VMEM((len(ws) * units, tokens), BF16)],
        compiler_params=pltpu.CompilerParams(vmem_limit_bytes=32 * 1024 * 1024),
        cost_estimate=pl.CostEstimate(
            flops=width + weight * 10**9, bytes_accessed=width, transcendentals=0
        ),
    )(*xs, *cs, *ws, *befores)


def input_kernel(n, *refs):
    parts, ws = refs[:n], refs[n:-4]
    outs = refs[-4:]
    w_all = jnp.concatenate([w[m] for w in ws for m in range(2)], axis=0)
    group = outs[0].shape[0]
    k = len(parts) // 2
    for i in range(4):
        half = parts[i // 2 * k : (i // 2 + 1) * k]
        a = jnp.concatenate([part[:, i % 2 * group : (i % 2 + 1) * group] for part in half], axis=0)
        total = lax.dot_general(a, w_all, TN, preferred_element_type=F32)
        outs[i][...] = total.astype(outs[i].dtype)


def input_parts(parts, ws):
    width = ws[0].shape[2]
    group = parts[0].shape[1] // 2
    vmem = pl.BlockSpec(memory_space=pltpu.VMEM)

    def kernel(*refs):
        input_kernel(len(parts), *refs)

    return pl.pallas_call(
        kernel,
        out_shape=[
            jax.ShapeDtypeStruct((group, width), kind) for kind in (F32, BF16, F32, BF16)
        ],
        in_specs=[vmem] * (len(parts) + len(ws)),
        out_specs=[vmem] * 4,
        compiler_params=pltpu.CompilerParams(vmem_limit_bytes=32 * 1024 * 1024),
        cost_estimate=pl.CostEstimate(
            flops=width, bytes_accessed=width, transcendentals=0
        ),
    )(*parts, *ws)


def stack_kernel(gate_up_ref, down_ref, out_ref):
    both = gate_up_ref[...].astype(F32)
    for m in range(2):
        out_ref[m] = both[:, m].astype(BF16)
    out_ref[2] = down_ref[...]


def stack_rows(gate_up, down_proj):
    vmem = pl.BlockSpec(memory_space=pltpu.VMEM)
    rows, width = down_proj.shape
    return pl.pallas_call(
        stack_kernel,
        out_shape=jax.ShapeDtypeStruct((3, rows, width), BF16),
        in_specs=[vmem] * 2,
        out_specs=vmem,
    )(gate_up, down_proj)


def body(activations, cotangent, gate_up, down_proj):
    x_z = swap_near(activations, Z)
    message = stack_rows(gate_up, down_proj)
    block1 = gather_block(swap_wrap(message, Z))
    o0 = gather_block(message)
    block1, c_own = lax.optimization_barrier((block1, cotangent))
    c_z = swap_near(c_own, Z)
    o1 = block1
    n0 = swap_second(o0, Y)
    r0 = swap_second(join(o0, n0), X)
    n1 = swap_second(o1, X)
    o1, x_z = lax.optimization_barrier((o1, x_z))
    w1 = swap_second(o1, Y)
    f1 = swap_second(n1, Y)
    xs, cs = [activations, swap_core(activations)], [cotangent, swap_core(cotangent)]

    near = [n1, o1, n0, o0]
    *g_near, a_near = grads(xs, cs, near, weight=3)
    x_z, c_z, a_near, w1 = lax.optimization_barrier((x_z, c_z, a_near, w1))
    xs_z, cs_z = [x_z, swap_core(x_z)], [c_z, swap_core(c_z)]
    f1, a_near = lax.optimization_barrier((f1, a_near))
    g_r1, a_r1 = grads(xs, cs, [w1, f1], joined=2, weight=6)

    g_r1, a_r1_z = grads(xs_z, cs_z, [w1, f1], [g_r1], joined=2)
    back1 = swap_second(g_r1, Y)
    r0, a_r1_z = lax.optimization_barrier((r0, a_r1_z))
    g_r0, a_r0 = grads(xs + xs_z, cs + cs_z, [r0])
    back0 = swap_second(g_r0, X)
    n1, a_r0 = lax.optimization_barrier((n1, a_r0))
    g_n1, g_o1, g_n0, g_o0, a_near_z = grads(xs_z, cs_z, [n1, o1, n0, o0], g_near)
    n = a_r0.shape[1] // 2
    parts = [a_r1, a_r0[:, :n], a_near, a_r1_z, a_r0[:, n:], a_near_z]
    own, pair, z_part, z_pair = input_parts(parts, [w1, f1, r0] + near)
    z_got, got = swap_core(z_pair), swap_core(pair)

    n = g_n1.shape[1]
    near1 = swap_second(add(g_n1, back1[:, n:]), X)
    back0, back1 = lax.optimization_barrier((back0, back1))
    near0 = swap_second(add(g_n0, back0[:, n:]), Y)
    back0, z_part = lax.optimization_barrier((back0, z_part))
    mine = own + got.astype(F32)
    z_part = swap_near((z_part + z_got.astype(F32)).astype(BF16), Z)

    def block_sum(own, back, near):
        return (own.astype(F32) + back.astype(F32) + near.astype(F32)).astype(BF16)

    terms1 = reduce_block(block_sum(g_o1, back1[:, :n], near1))
    total1 = added(terms1).astype(BF16)
    total0 = added(reduce_block(block_sum(g_o0, back0[:, :n], near0)))
    grad_input = (mine + z_part.astype(F32)).astype(BF16)
    total = total0 + swap_wrap(total1, Z).astype(F32)
    return (grad_input, total.transpose(1, 0, 2))


def solution(mesh):
    in_specs = (
        P(("node", "local"), None),
        P(("node", "local"), None),
        P(("node", "local"), None, None),
        P(("node", "local"), None),
    )
    out_specs = (P(("node", "local"), None), P(("node", "local"), None, None))
    return jax.shard_map(body, mesh=mesh, in_specs=in_specs, out_specs=out_specs, check_vma=False)
```

```python
import jax
import jax.numpy as jnp
from jax import lax
from jax.experimental import pallas as pl
from jax.experimental.pallas import tpu as pltpu
from jax.sharding import PartitionSpec as P

AXES = ("node", "local")
X, Y, Z = 0, 1, 2
RING = 4
DEVICES = 128
TILE = 256
BF16 = jnp.bfloat16
F32 = jnp.float32
NT = (((1,), (1,)), ((), ()))
TN = (((0,), (0,)), ((), ()))


def place(device):
    return [device // 64 * 2 + device // 2 % 2, device // 16 % 4, device // 4 % 4, device % 2]


def index(x, y, z, core):
    return (x // 2) * 64 + y * 16 + z * 4 + (x % 2) * 2 + core


def swap(value, axis, wrap):
    pairs = []
    for device in range(DEVICES):
        there = place(device)
        there[axis] = RING - 1 - there[axis] if wrap(there[3]) else there[axis] ^ 1
        pairs.append((device, index(*there)))
    return lax.ppermute(value, AXES, pairs)


def swap_first(value, axis, part):
    return swap(value, axis, lambda core: (core + part) % 2 == 1)


def swap_second(value, axis, part):
    return swap(value, axis, lambda core: (core + part) % 2 == 0)


def swap_near(value, axis):
    return swap(value, axis, lambda core: False)


def swap_wrap(value, axis):
    return swap(value, axis, lambda core: True)


def swap_corner(value, part):
    pairs = []
    for device in range(DEVICES):
        there = place(device)
        for axis in (X, Y):
            there[axis] = RING - 1 - there[axis] if (there[3] + part) % 2 == 1 else there[axis] ^ 1
        pairs.append((device, index(*there)))
    return lax.ppermute(value, AXES, pairs)


def swap_core(value):
    return lax.ppermute(value, AXES, [(d, d ^ 1) for d in range(DEVICES)])


def add(a, b):
    return (a.astype(F32) + b.astype(F32)).astype(BF16)


def join(*blocks):
    return jnp.concatenate(blocks, axis=1)


def gather_block(message, part):
    return join(
        message, swap_first(message, Y, part), swap_first(message, X, part), swap_corner(message, part)
    )


def reduce_block(block, part):
    n = block.shape[1] // 4
    own, along_y, along_x, corner = (block[:, i * n : (i + 1) * n] for i in range(4))
    return own, swap_first(along_y, Y, part), swap_first(along_x, X, part), swap_corner(corner, part)


def added(terms):
    return sum(term.astype(F32) for term in terms)


def rows_of(refs, start, stop, cols=slice(None)):
    parts = []
    for ref in refs:
        n = ref.shape[0]
        if start < n and stop > 0:
            parts.append(ref[max(start, 0) : min(stop, n), cols])
        start, stop = start - n, stop - n
    return parts[0] if len(parts) == 1 else jnp.concatenate(parts, axis=0)


def grads_kernel(n, m, parts, joined, *refs):
    xs, cs, refs = refs[:n], refs[n : n + m], refs[n + m :]
    a_ref, hid = refs[-2:]
    outs = parts // joined
    ws, befores, gs = refs[:parts], refs[parts : -2 - outs], refs[-2 - outs : -2]
    units, width = ws[0].shape[1:]
    gu = jnp.concatenate([w[m] for w in ws for m in range(2)], axis=0)
    down = jnp.concatenate([w[2] for w in ws], axis=0)
    tokens = hid.shape[1]
    for t in range(tokens // TILE):
        rows = slice(t * TILE, (t + 1) * TILE)
        x = rows_of(xs, t * TILE, (t + 1) * TILE)
        c = rows_of(cs, t * TILE, (t + 1) * TILE)
        z = lax.dot_general(gu, x, NT, preferred_element_type=F32)
        gh = lax.dot_general(down, c, NT, preferred_element_type=F32)
        for p in range(parts):
            gate = z[2 * p * units : (2 * p + 1) * units]
            up = z[(2 * p + 1) * units : (2 * p + 2) * units]
            grad = gh[p * units : (p + 1) * units]
            sg = 1.0 / (1.0 + jnp.exp(-gate))
            silu = gate * sg
            hid[p * units : (p + 1) * units, rows] = (silu * up).astype(BF16)
            slope = sg + silu * (1.0 - sg)
            a_ref[2 * p * units : (2 * p + 1) * units, rows] = (grad * up * slope).astype(BF16)
            a_ref[(2 * p + 1) * units : (2 * p + 2) * units, rows] = (grad * silu).astype(BF16)
    for k in range(width // TILE):
        cols = slice(k * TILE, (k + 1) * TILE)
        x = rows_of(xs, 0, tokens, cols)
        c = rows_of(cs, 0, tokens, cols)
        d_gu = jnp.dot(a_ref[...], x, preferred_element_type=F32)
        d_down = jnp.dot(hid[...], c, preferred_element_type=F32)
        for p in range(parts):
            g, before = gs[p // joined], befores[p // joined] if befores else None
            to = slice(p % joined * units, (p % joined + 1) * units)
            for m in range(3):
                source, row = (d_down, p) if m == 2 else (d_gu, 2 * p + m)
                sums = source[row * units : (row + 1) * units]
                if before is not None:
                    sums = sums + before[m, to, cols].astype(F32)
                g[m, to, cols] = sums.astype(BF16)


def grads(xs, cs, ws, befores=(), joined=1, weight=0):
    units, width = ws[0].shape[1:]
    tokens = sum(x.shape[0] for x in xs)
    vmem = pl.BlockSpec(memory_space=pltpu.VMEM)

    def kernel(*refs):
        grads_kernel(len(xs), len(cs), len(ws), joined, *refs)

    return pl.pallas_call(
        kernel,
        out_shape=[jax.ShapeDtypeStruct((3, joined * units, width), BF16)] * (len(ws) // joined)
        + [jax.ShapeDtypeStruct((2 * len(ws) * units, tokens), BF16)],
        in_specs=[vmem] * (len(xs) + len(cs) + len(ws) + len(befores)),
        out_specs=[vmem] * (len(ws) // joined + 1),
        scratch_shapes=[pltpu.VMEM((len(ws) * units, tokens), BF16)],
        compiler_params=pltpu.CompilerParams(vmem_limit_bytes=32 * 1024 * 1024),
        cost_estimate=pl.CostEstimate(
            flops=width + weight * 10**9, bytes_accessed=width, transcendentals=0
        ),
    )(*xs, *cs, *ws, *befores)


def input_kernel(n, *refs):
    parts, ws = refs[:n], refs[n:-4]
    outs = refs[-4:]
    w_all = jnp.concatenate([w[m] for w in ws for m in range(2)], axis=0)
    group = outs[0].shape[0]
    k = len(parts) // 2
    for i in range(4):
        half = parts[i // 2 * k : (i // 2 + 1) * k]
        a = jnp.concatenate([part[:, i % 2 * group : (i % 2 + 1) * group] for part in half], axis=0)
        total = lax.dot_general(a, w_all, TN, preferred_element_type=F32)
        outs[i][...] = total.astype(outs[i].dtype)


def input_parts(parts, ws):
    width = ws[0].shape[2]
    group = parts[0].shape[1] // 2
    vmem = pl.BlockSpec(memory_space=pltpu.VMEM)

    def kernel(*refs):
        input_kernel(len(parts), *refs)

    return pl.pallas_call(
        kernel,
        out_shape=[
            jax.ShapeDtypeStruct((group, width), kind) for kind in (F32, BF16, F32, BF16)
        ],
        in_specs=[vmem] * (len(parts) + len(ws)),
        out_specs=[vmem] * 4,
        compiler_params=pltpu.CompilerParams(vmem_limit_bytes=32 * 1024 * 1024),
        cost_estimate=pl.CostEstimate(
            flops=width, bytes_accessed=width, transcendentals=0
        ),
    )(*parts, *ws)


def body(activations, cotangent, gate_up, down_proj):
    x_z = swap_near(activations, Z)
    message = jnp.concatenate([gate_up.transpose(1, 0, 2), down_proj[None]], axis=0)
    message = lax.optimization_barrier(message)
    block1 = gather_block(swap_wrap(message, Z), 1)
    o0 = gather_block(message, 0)
    block1, c_own = lax.optimization_barrier((block1, cotangent))
    c_z = swap_near(c_own, Z)
    o1 = block1
    n0 = swap_second(o0, Y, 0)
    r0 = swap_second(join(o0, n0), X, 0)
    n1 = swap_second(o1, X, 1)
    o1, x_z = lax.optimization_barrier((o1, x_z))
    w1 = swap_second(o1, Y, 1)
    f1 = swap_second(n1, Y, 1)
    xs, cs = [activations, swap_core(activations)], [cotangent, swap_core(cotangent)]

    near = [n1, o1, n0, o0]
    *g_near, a_near = grads(xs, cs, near, weight=3)
    x_z, c_z, a_near, w1 = lax.optimization_barrier((x_z, c_z, a_near, w1))
    xs_z, cs_z = [x_z, swap_core(x_z)], [c_z, swap_core(c_z)]
    f1, a_near = lax.optimization_barrier((f1, a_near))
    g_r1, a_r1 = grads(xs, cs, [w1, f1], joined=2, weight=6)

    g_r1, a_r1_z = grads(xs_z, cs_z, [w1, f1], [g_r1], joined=2)
    back1 = swap_second(g_r1, Y, 1)
    r0, a_r1_z = lax.optimization_barrier((r0, a_r1_z))
    g_r0, a_r0 = grads(xs + xs_z, cs + cs_z, [r0])
    back0 = swap_second(g_r0, X, 0)
    n1, a_r0 = lax.optimization_barrier((n1, a_r0))
    g_n1, g_o1, g_n0, g_o0, a_near_z = grads(xs_z, cs_z, [n1, o1, n0, o0], g_near)
    n = a_r0.shape[1] // 2
    parts = [a_r1, a_r0[:, :n], a_near, a_r1_z, a_r0[:, n:], a_near_z]
    own, pair, z_part, z_pair = input_parts(parts, [w1, f1, r0] + near)
    z_got, got = swap_core(z_pair), swap_core(pair)

    n = g_n1.shape[1]
    near1 = swap_second(add(g_n1, back1[:, n:]), X, 1)
    back0, back1 = lax.optimization_barrier((back0, back1))
    near0 = swap_second(add(g_n0, back0[:, n:]), Y, 0)
    back0, z_part = lax.optimization_barrier((back0, z_part))
    mine = own + got.astype(F32)
    z_part = swap_near((z_part + z_got.astype(F32)).astype(BF16), Z)

    def block_sum(own, back, near):
        return (own.astype(F32) + back.astype(F32) + near.astype(F32)).astype(BF16)

    terms1 = reduce_block(block_sum(g_o1, back1[:, :n], near1), 1)
    total1 = added(terms1).astype(BF16)
    total0 = added(reduce_block(block_sum(g_o0, back0[:, :n], near0), 0))
    grad_input = (mine + z_part.astype(F32)).astype(BF16)
    total = total0 + swap_wrap(total1, Z).astype(F32)
    return (grad_input, total.transpose(1, 0, 2))


def solution(mesh):
    in_specs = (
        P(("node", "local"), None),
        P(("node", "local"), None),
        P(("node", "local"), None, None),
        P(("node", "local"), None),
    )
    out_specs = (P(("node", "local"), None), P(("node", "local"), None, None))
    return jax.shard_map(body, mesh=mesh, in_specs=in_specs, out_specs=out_specs, check_vma=False)
```

```python
import jax
import jax.numpy as jnp
from jax import lax
from jax.experimental import pallas as pl
from jax.experimental.pallas import tpu as pltpu
from jax.sharding import PartitionSpec as P

AXES = ("node", "local")
X, Y, Z = 0, 1, 2
RING = 4
DEVICES = 128
TILE = 256
BF16 = jnp.bfloat16
F32 = jnp.float32
NT = (((1,), (1,)), ((), ()))
TN = (((0,), (0,)), ((), ()))


def place(device):
    return [device // 64 * 2 + device // 2 % 2, device // 16 % 4, device // 4 % 4, device % 2]


def index(x, y, z, core):
    return (x // 2) * 64 + y * 16 + z * 4 + (x % 2) * 2 + core


def swap(value, axis, wrap):
    pairs = []
    for device in range(DEVICES):
        there = place(device)
        there[axis] = RING - 1 - there[axis] if wrap(there[3]) else there[axis] ^ 1
        pairs.append((device, index(*there)))
    return lax.ppermute(value, AXES, pairs)


def swap_first(value, axis):
    return swap(value, axis, lambda core: core == 1)


def swap_second(value, axis):
    return swap(value, axis, lambda core: core == 0)


def swap_near(value, axis):
    return swap(value, axis, lambda core: False)


def swap_wrap(value, axis):
    return swap(value, axis, lambda core: True)


def swap_corner(value):
    pairs = []
    for device in range(DEVICES):
        there = place(device)
        for axis in (X, Y):
            there[axis] = RING - 1 - there[axis] if there[3] == 1 else there[axis] ^ 1
        pairs.append((device, index(*there)))
    return lax.ppermute(value, AXES, pairs)


def swap_core(value):
    return lax.ppermute(value, AXES, [(d, d ^ 1) for d in range(DEVICES)])


def add(a, b):
    return (a.astype(F32) + b.astype(F32)).astype(BF16)


def join(*blocks):
    return jnp.concatenate(blocks, axis=1)


def gather_block(message):
    return join(message, swap_first(message, Y), swap_first(message, X), swap_corner(message))


def reduce_block(block):
    n = block.shape[1] // 4
    own, along_y, along_x, corner = (block[:, i * n : (i + 1) * n] for i in range(4))
    total = own.astype(F32) + swap_first(along_y, Y).astype(F32)
    return total + swap_first(along_x, X).astype(F32) + swap_corner(corner).astype(F32)


def summed(own, back, near):
    return (own.astype(F32) + back.astype(F32) + near.astype(F32)).astype(BF16)


def rows_of(refs, start, stop, cols=slice(None)):
    parts = []
    for ref in refs:
        n = ref.shape[0]
        if start < n and stop > 0:
            parts.append(ref[max(start, 0) : min(stop, n), cols])
        start, stop = start - n, stop - n
    return parts[0] if len(parts) == 1 else jnp.concatenate(parts, axis=0)


def grads_kernel(n, *refs):
    xs, cs, refs = refs[:n], refs[n : 2 * n], refs[2 * n :]
    a_ref, hid = refs[-2:]
    parts = len(refs) // 2 - 1
    ws, gs = refs[:parts], refs[parts:-2]
    units, width = ws[0].shape[1:]
    gu = jnp.concatenate([w[m] for w in ws for m in range(2)], axis=0)
    down = jnp.concatenate([w[2] for w in ws], axis=0)
    tokens = hid.shape[1]
    for t in range(tokens // TILE):
        rows = slice(t * TILE, (t + 1) * TILE)
        x = rows_of(xs, t * TILE, (t + 1) * TILE)
        c = rows_of(cs, t * TILE, (t + 1) * TILE)
        z = lax.dot_general(gu, x, NT, preferred_element_type=F32)
        gh = lax.dot_general(down, c, NT, preferred_element_type=F32)
        for p in range(parts):
            gate = z[2 * p * units : (2 * p + 1) * units]
            up = z[(2 * p + 1) * units : (2 * p + 2) * units]
            grad = gh[p * units : (p + 1) * units]
            sg = 1.0 / (1.0 + jnp.exp(-gate))
            silu = gate * sg
            hid[p * units : (p + 1) * units, rows] = (silu * up).astype(BF16)
            slope = sg + silu * (1.0 - sg)
            a_ref[2 * p * units : (2 * p + 1) * units, rows] = (grad * up * slope).astype(BF16)
            a_ref[(2 * p + 1) * units : (2 * p + 2) * units, rows] = (grad * silu).astype(BF16)
    for k in range(width // TILE):
        cols = slice(k * TILE, (k + 1) * TILE)
        x = rows_of(xs, 0, tokens, cols)
        c = rows_of(cs, 0, tokens, cols)
        d_gu = jnp.dot(a_ref[...], x, preferred_element_type=F32).astype(BF16)
        d_down = jnp.dot(hid[...], c, preferred_element_type=F32).astype(BF16)
        for p, g in enumerate(gs):
            for m in range(2):
                g[m, :, cols] = d_gu[(2 * p + m) * units : (2 * p + m + 1) * units]
            g[2, :, cols] = d_down[p * units : (p + 1) * units]


def grads(xs, cs, ws):
    units, width = ws[0].shape[1:]
    tokens = sum(x.shape[0] for x in xs)
    vmem = pl.BlockSpec(memory_space=pltpu.VMEM)

    def kernel(*refs):
        grads_kernel(len(xs), *refs)

    return pl.pallas_call(
        kernel,
        out_shape=[jax.ShapeDtypeStruct(w.shape, BF16) for w in ws]
        + [jax.ShapeDtypeStruct((2 * len(ws) * units, tokens), BF16)],
        in_specs=[vmem] * (2 * len(xs) + len(ws)),
        out_specs=[vmem] * (len(ws) + 1),
        scratch_shapes=[pltpu.VMEM((len(ws) * units, tokens), BF16)],
        compiler_params=pltpu.CompilerParams(vmem_limit_bytes=32 * 1024 * 1024),
        cost_estimate=pl.CostEstimate(
            flops=width, bytes_accessed=width, transcendentals=0
        ),
    )(*xs, *cs, *ws)


def input_kernel(n, *refs):
    parts, ws = refs[:n], refs[n:-3]
    own_ref, z_ref, pair_ref = refs[-3:]
    w_all = jnp.concatenate([w[m] for w in ws for m in range(2)], axis=0)
    group = own_ref.shape[0]
    for i in range(4):
        cols = slice(i * group, (i + 1) * group)
        a = jnp.concatenate([part[:, cols] for part in parts], axis=0)
        total = lax.dot_general(a, w_all, TN, preferred_element_type=F32)
        if i == 0:
            own_ref[...] = total
        elif i == 2:
            z_ref[...] = total
        else:
            pair_ref[i // 2] = total.astype(BF16)


def input_parts(parts, ws):
    units, width = ws[0].shape[1:]
    group = parts[0].shape[1] // 4
    vmem = pl.BlockSpec(memory_space=pltpu.VMEM)

    def kernel(*refs):
        input_kernel(len(parts), *refs)

    return pl.pallas_call(
        kernel,
        out_shape=[
            jax.ShapeDtypeStruct((group, width), F32),
            jax.ShapeDtypeStruct((group, width), F32),
            jax.ShapeDtypeStruct((2, group, width), BF16),
        ],
        in_specs=[vmem] * (len(parts) + len(ws)),
        out_specs=[vmem] * 3,
        compiler_params=pltpu.CompilerParams(vmem_limit_bytes=32 * 1024 * 1024),
        cost_estimate=pl.CostEstimate(
            flops=width, bytes_accessed=width, transcendentals=0
        ),
    )(*parts, *ws)


def body(activations, cotangent, gate_up, down_proj):
    x_z = swap_near(activations, Z)
    message = jnp.concatenate([gate_up.transpose(1, 0, 2), down_proj[None]], axis=0)
    message = lax.optimization_barrier(message)
    other = swap_wrap(message, Z)
    block0 = gather_block(message)
    block1 = gather_block(other)
    block1, c_own = lax.optimization_barrier((block1, cotangent))
    gated, x_z = lax.optimization_barrier((block1, x_z))
    c_z = swap_near(c_own, Z)
    j0 = join(block0, swap_second(block0, Y))
    j1 = join(block1, swap_second(gated, X))
    r0, r1 = swap_second(j0, X), swap_second(j1, Y)
    xs = [activations, swap_core(activations), x_z, swap_core(x_z)]
    cs = [cotangent, swap_core(cotangent), c_z, swap_core(c_z)]

    g_r0, a_r0 = grads(xs, cs, [r0])
    back0 = swap_second(g_r0, X)
    g_r1, a_r1 = grads(xs, cs, [r1])
    back1 = swap_second(g_r1, Y)
    j0, j1, a_r1 = lax.optimization_barrier((j0, j1, a_r1))
    g_j0, g_j1, a_j = grads(xs, cs, [j0, j1])

    own, z_part, pair = input_parts([a_r0, a_r1, a_j], [r0, r1, j0, j1])
    got = swap_core(pair)
    n = back0.shape[1] // 2
    give0, give1 = add(g_j0[:, n:], back0[:, n:]), add(g_j1[:, n:], back1[:, n:])
    give0, give1, z_part = lax.optimization_barrier((give0, give1, z_part))
    mine = own + got[0].astype(F32)
    z_part = swap_near((z_part + got[1].astype(F32)).astype(BF16), Z)

    total1 = reduce_block(summed(g_j1[:, :n], back1[:, :n], swap_second(give1, X))).astype(BF16)
    grad_input = (mine + z_part.astype(F32)).astype(BF16)
    total0 = reduce_block(summed(g_j0[:, :n], back0[:, :n], swap_second(give0, Y)))
    total = total0 + swap_wrap(total1, Z).astype(F32)
    return (grad_input, total.transpose(1, 0, 2))


def solution(mesh):
    in_specs = (
        P(("node", "local"), None),
        P(("node", "local"), None),
        P(("node", "local"), None, None),
        P(("node", "local"), None),
    )
    out_specs = (P(("node", "local"), None), P(("node", "local"), None, None))
    return jax.shard_map(body, mesh=mesh, in_specs=in_specs, out_specs=out_specs, check_vma=False)
```

```python
import jax
import jax.numpy as jnp
from jax import lax
from jax.experimental import pallas as pl
from jax.experimental.pallas import tpu as pltpu
from jax.sharding import PartitionSpec as P

AXES = ("node", "local")
X, Y, Z = 0, 1, 2
RING = 4
DEVICES = 128
TILE = 256
BF16 = jnp.bfloat16
F32 = jnp.float32
NT = (((1,), (1,)), ((), ()))
TN = (((0,), (0,)), ((), ()))


def place(device):
    return [device // 64 * 2 + device // 2 % 2, device // 16 % 4, device // 4 % 4, device % 2]


def index(x, y, z, core):
    return (x // 2) * 64 + y * 16 + z * 4 + (x % 2) * 2 + core


def swap(value, axis, wrap):
    pairs = []
    for device in range(DEVICES):
        there = place(device)
        there[axis] = RING - 1 - there[axis] if wrap(there[3]) else there[axis] ^ 1
        pairs.append((device, index(*there)))
    return lax.ppermute(value, AXES, pairs)


def swap_first(value, axis):
    return swap(value, axis, lambda core: core == 1)


def swap_second(value, axis):
    return swap(value, axis, lambda core: core == 0)


def swap_near(value, axis):
    return swap(value, axis, lambda core: False)


def swap_wrap(value, axis):
    return swap(value, axis, lambda core: True)


def swap_corner(value):
    pairs = []
    for device in range(DEVICES):
        there = place(device)
        for axis in (X, Y):
            there[axis] = RING - 1 - there[axis] if there[3] == 1 else there[axis] ^ 1
        pairs.append((device, index(*there)))
    return lax.ppermute(value, AXES, pairs)


def swap_core(value):
    return lax.ppermute(value, AXES, [(d, d ^ 1) for d in range(DEVICES)])


def add(a, b):
    return (a.astype(F32) + b.astype(F32)).astype(BF16)


def join(*blocks):
    return jnp.concatenate(blocks, axis=1)


def gather_block(message):
    return join(message, swap_first(message, Y), swap_first(message, X), swap_corner(message))


def reduce_block(block):
    n = block.shape[1] // 4
    own, along_y, along_x, corner = (block[:, i * n : (i + 1) * n] for i in range(4))
    return own, swap_first(along_y, Y), swap_first(along_x, X), swap_corner(corner)


def added(terms):
    return sum(term.astype(F32) for term in terms)


def rows_of(refs, start, stop, cols=slice(None)):
    parts = []
    for ref in refs:
        n = ref.shape[0]
        if start < n and stop > 0:
            parts.append(ref[max(start, 0) : min(stop, n), cols])
        start, stop = start - n, stop - n
    return parts[0] if len(parts) == 1 else jnp.concatenate(parts, axis=0)


def grads_kernel(n, m, parts, joined, *refs):
    xs, cs, refs = refs[:n], refs[n : n + m], refs[n + m :]
    a_ref, hid = refs[-2:]
    outs = parts // joined
    ws, befores, gs = refs[:parts], refs[parts : -2 - outs], refs[-2 - outs : -2]
    units, width = ws[0].shape[1:]
    gu = jnp.concatenate([w[m] for w in ws for m in range(2)], axis=0)
    down = jnp.concatenate([w[2] for w in ws], axis=0)
    tokens = hid.shape[1]
    for t in range(tokens // TILE):
        rows = slice(t * TILE, (t + 1) * TILE)
        x = rows_of(xs, t * TILE, (t + 1) * TILE)
        c = rows_of(cs, t * TILE, (t + 1) * TILE)
        z = lax.dot_general(gu, x, NT, preferred_element_type=F32)
        gh = lax.dot_general(down, c, NT, preferred_element_type=F32)
        for p in range(parts):
            gate = z[2 * p * units : (2 * p + 1) * units]
            up = z[(2 * p + 1) * units : (2 * p + 2) * units]
            grad = gh[p * units : (p + 1) * units]
            sg = 1.0 / (1.0 + jnp.exp(-gate))
            silu = gate * sg
            hid[p * units : (p + 1) * units, rows] = (silu * up).astype(BF16)
            slope = sg + silu * (1.0 - sg)
            a_ref[2 * p * units : (2 * p + 1) * units, rows] = (grad * up * slope).astype(BF16)
            a_ref[(2 * p + 1) * units : (2 * p + 2) * units, rows] = (grad * silu).astype(BF16)
    for k in range(width // TILE):
        cols = slice(k * TILE, (k + 1) * TILE)
        x = rows_of(xs, 0, tokens, cols)
        c = rows_of(cs, 0, tokens, cols)
        d_gu = jnp.dot(a_ref[...], x, preferred_element_type=F32)
        d_down = jnp.dot(hid[...], c, preferred_element_type=F32)
        for p in range(parts):
            g, before = gs[p // joined], befores[p // joined] if befores else None
            to = slice(p % joined * units, (p % joined + 1) * units)
            for m in range(3):
                source, row = (d_down, p) if m == 2 else (d_gu, 2 * p + m)
                sums = source[row * units : (row + 1) * units]
                if before is not None:
                    sums = sums + before[m, to, cols].astype(F32)
                g[m, to, cols] = sums.astype(BF16)


def grads(xs, cs, ws, befores=(), joined=1, weight=0):
    units, width = ws[0].shape[1:]
    tokens = sum(x.shape[0] for x in xs)
    vmem = pl.BlockSpec(memory_space=pltpu.VMEM)

    def kernel(*refs):
        grads_kernel(len(xs), len(cs), len(ws), joined, *refs)

    return pl.pallas_call(
        kernel,
        out_shape=[jax.ShapeDtypeStruct((3, joined * units, width), BF16)] * (len(ws) // joined)
        + [jax.ShapeDtypeStruct((2 * len(ws) * units, tokens), BF16)],
        in_specs=[vmem] * (len(xs) + len(cs) + len(ws) + len(befores)),
        out_specs=[vmem] * (len(ws) // joined + 1),
        scratch_shapes=[pltpu.VMEM((len(ws) * units, tokens), BF16)],
        compiler_params=pltpu.CompilerParams(vmem_limit_bytes=32 * 1024 * 1024),
        cost_estimate=pl.CostEstimate(
            flops=width + weight * 10**9, bytes_accessed=width, transcendentals=0
        ),
    )(*xs, *cs, *ws, *befores)


def input_kernel(n, *refs):
    parts, ws = refs[:n], refs[n:-4]
    outs = refs[-4:]
    w_all = jnp.concatenate([w[m] for w in ws for m in range(2)], axis=0)
    group = outs[0].shape[0]
    k = len(parts) // 2
    for i in range(4):
        half = parts[i // 2 * k : (i // 2 + 1) * k]
        a = jnp.concatenate([part[:, i % 2 * group : (i % 2 + 1) * group] for part in half], axis=0)
        total = lax.dot_general(a, w_all, TN, preferred_element_type=F32)
        outs[i][...] = total.astype(outs[i].dtype)


def input_parts(parts, ws):
    width = ws[0].shape[2]
    group = parts[0].shape[1] // 2
    vmem = pl.BlockSpec(memory_space=pltpu.VMEM)

    def kernel(*refs):
        input_kernel(len(parts), *refs)

    return pl.pallas_call(
        kernel,
        out_shape=[
            jax.ShapeDtypeStruct((group, width), kind) for kind in (F32, BF16, F32, BF16)
        ],
        in_specs=[vmem] * (len(parts) + len(ws)),
        out_specs=[vmem] * 4,
        compiler_params=pltpu.CompilerParams(vmem_limit_bytes=32 * 1024 * 1024),
        cost_estimate=pl.CostEstimate(
            flops=width, bytes_accessed=width, transcendentals=0
        ),
    )(*parts, *ws)


def body(activations, cotangent, gate_up, down_proj):
    x_z = swap_near(activations, Z)
    message = jnp.concatenate([gate_up.transpose(1, 0, 2), down_proj[None]], axis=0)
    message = lax.optimization_barrier(message)
    block1 = gather_block(swap_wrap(message, Z))
    o0 = gather_block(message)
    block1, c_own = lax.optimization_barrier((block1, cotangent))
    c_z = swap_near(c_own, Z)
    o1 = block1
    n0 = swap_second(o0, Y)
    r0 = swap_second(join(o0, n0), X)
    n1 = swap_second(o1, X)
    o1, x_z = lax.optimization_barrier((o1, x_z))
    w1 = swap_second(o1, Y)
    f1 = swap_second(n1, Y)
    xs, cs = [activations, swap_core(activations)], [cotangent, swap_core(cotangent)]

    near = [n1, o1, n0, o0]
    *g_near, a_near = grads(xs, cs, near, weight=3)
    x_z, c_z, a_near, w1 = lax.optimization_barrier((x_z, c_z, a_near, w1))
    xs_z, cs_z = [x_z, swap_core(x_z)], [c_z, swap_core(c_z)]
    f1, a_near = lax.optimization_barrier((f1, a_near))
    g_r1, a_r1 = grads(xs, cs, [w1, f1], joined=2, weight=6)

    g_r1, a_r1_z = grads(xs_z, cs_z, [w1, f1], [g_r1], joined=2)
    back1 = swap_second(g_r1, Y)
    r0, a_r1_z = lax.optimization_barrier((r0, a_r1_z))
    g_r0, a_r0 = grads(xs + xs_z, cs + cs_z, [r0])
    back0 = swap_second(g_r0, X)
    n1, a_r0 = lax.optimization_barrier((n1, a_r0))
    g_n1, g_o1, g_n0, g_o0, a_near_z = grads(xs_z, cs_z, [n1, o1, n0, o0], g_near)
    n = a_r0.shape[1] // 2
    parts = [a_r1, a_r0[:, :n], a_near, a_r1_z, a_r0[:, n:], a_near_z]
    own, pair, z_part, z_pair = input_parts(parts, [w1, f1, r0] + near)
    z_got, got = swap_core(z_pair), swap_core(pair)

    n = g_n1.shape[1]
    near1 = swap_second(add(g_n1, back1[:, n:]), X)
    back0, back1 = lax.optimization_barrier((back0, back1))
    near0 = swap_second(add(g_n0, back0[:, n:]), Y)
    back0, z_part = lax.optimization_barrier((back0, z_part))
    mine = own + got.astype(F32)
    z_part = swap_near((z_part + z_got.astype(F32)).astype(BF16), Z)

    def block_sum(own, back, near):
        return (own.astype(F32) + back.astype(F32) + near.astype(F32)).astype(BF16)

    terms1 = reduce_block(block_sum(g_o1, back1[:, :n], near1))
    total1 = added(terms1).astype(BF16)
    total0 = added(reduce_block(block_sum(g_o0, back0[:, :n], near0)))
    grad_input = (mine + z_part.astype(F32)).astype(BF16)
    total = total0 + swap_wrap(total1, Z).astype(F32)
    return (grad_input, total.transpose(1, 0, 2))


def solution(mesh):
    in_specs = (
        P(("node", "local"), None),
        P(("node", "local"), None),
        P(("node", "local"), None, None),
        P(("node", "local"), None),
    )
    out_specs = (P(("node", "local"), None), P(("node", "local"), None, None))
    return jax.shard_map(body, mesh=mesh, in_specs=in_specs, out_specs=out_specs, check_vma=False)
```
